32 devices in a mesh: seq: 8 (over z, y), fsdp: 4 (over x, core).
Axes of the slice: x: 2, y: 2, z: 4, core: 2. Of those that a mesh axis runs over, the one named last changes fastest.
Arguments:
- inputs: float32 [8, 56, 28, 512], P('fsdp', 'seq'), may hold values from -6 to 6
- out_grad: float32 [8, 56, 28, 512], P('fsdp', 'seq'), may hold values from -6 to 6
- regions: int32 [56, 28], P('seq'), may hold values from 0 to 127, as said below
- rel_index: int32 [49, 49], replicated, may hold values from 0 to 168, as said below
- qkv_weight: float32 [512, 1536], P('fsdp'), may hold values from -0.25 to 0.25
- qkv_first: float32 [512, 1536], P('fsdp'), may hold values from -80 to 80
- qkv_second: float32 [512, 1536], P('fsdp'), may hold values from 12.544 to 50.176
- proj_weight: float32 [512, 512], P('fsdp'), may hold values from -0.75 to 0.75
- proj_first: float32 [512, 512], P('fsdp'), may hold values from -40 to 40
- proj_second: float32 [512, 512], P('fsdp'), may hold values from 3.136 to 12.544
- up_weight: float32 [512, 2048], P('fsdp'), may hold values from -0.25 to 0.25
- up_first: float32 [512, 2048], P('fsdp'), may hold values from -24 to 24
- up_second: float32 [512, 2048], P('fsdp'), may hold values from 1.12896 to 4.51584
- down_weight: float32 [2048, 512], P('fsdp'), may hold values from -0.125 to 0.125
- down_first: float32 [2048, 512], P('fsdp'), may hold values from -48 to 48
- down_second: float32 [2048, 512], P('fsdp'), may hold values from 5.0176 to 21.3248
- vectors: float32 [6144], replicated, may hold values from -0.6 to 1.4, as said below
- vectors_first: float32 [6144], replicated, may hold values from -64 to 64
- vectors_second: float32 [6144], replicated, may hold values from 2.5088 to 50.176
- bias_table: float32 [16, 169], replicated, may hold values from -5 to 5
- table_first: float32 [16, 169], replicated, may hold values from -80 to 80
- table_second: float32 [16, 169], replicated, may hold values from 12.544 to 50.176
Outputs:
- block_out: float32 [8, 56, 28, 512], P('fsdp', 'seq')
- input_grad: float32 [8, 56, 28, 512], P('fsdp', 'seq')
- new_qkv: float32 [512, 1536], P('fsdp')
- new_qkv_first: float32 [512, 1536], P('fsdp')
- new_qkv_second: float32 [512, 1536], P('fsdp')
- new_proj: float32 [512, 512], P('fsdp')
- new_proj_first: float32 [512, 512], P('fsdp')
- new_proj_second: float32 [512, 512], P('fsdp')
- new_up: float32 [512, 2048], P('fsdp')
- new_up_first: float32 [512, 2048], P('fsdp')
- new_up_second: float32 [512, 2048], P('fsdp')
- new_down: float32 [2048, 512], P('fsdp')
- new_down_first: float32 [2048, 512], P('fsdp')
- new_down_second: float32 [2048, 512], P('fsdp')
- new_vectors: float32 [6144], replicated
- new_vectors_first: float32 [6144], replicated
- new_vectors_second: float32 [6144], replicated
- new_table: float32 [16, 169], replicated
- new_table_first: float32 [16, 169], replicated
- new_table_second: float32 [16, 169], replicated
The draws below stay inside these ranges and needn't reach their ends.
Inputs may be any that keep to these rules, and one draw needn't show every extreme that they name: `regions`: label at (i, j) is 2 * 4 * u + v with u = 2 (i // 7) + (1 if i mod 7 is at least a cut of that row of windows, else 0), v likewise from j and a cut of that column of windows. Each row and column of windows has its own cut; cuts of the first and last ones lie in 1 to 6, the others in 0 to 6. `rel_index`: entry (p, q) depends only on the offset between window positions p and q (position 7 r + c); distinct offsets have distinct entries. `vectors`: the two norms' gains lie in 0.6 to 1.4; the biases in -0.6 to 0.6.
All inputs are finite; a program needn't handle non-finite values.
Results may differ from the reference program's by a relative error of at most 0.02.
Values may be sent and summed in bfloat16 or wider, within the bound.
A program may use at most 128 MiB of HBM per device.

```python
import math
import jax
import jax.numpy as jnp
from jax import lax

D = 512
FF = 2048
HEAD_DIM = 32
WIN = 7
SHIFT = 3
STEP = 10
WCOLS = 4
HEADS = 16
W = 28
H = 56
IMAGES = 8
TOKENS = 12544
PAIRS = 49
TAB = 169
VEC = 6144


def part_labels(key, count):
    blocks = count // WIN
    inner = jax.random.randint(key, (blocks,), 0, WIN)
    edge_key = jax.random.fold_in(key, 5)
    edges = jax.random.randint(edge_key, (blocks,), 1, WIN)
    block_place = jnp.arange(blocks)
    cuts = jnp.where((block_place == 0) | (block_place == blocks - 1), edges, inner)
    place = jnp.arange(count)
    block_of = place // WIN
    cut_here = jnp.sum(jnp.where(block_of[:, None] == block_place[None, :], cuts[None, :], 0), axis=1)
    return 2 * block_of + (place % WIN >= cut_here).astype(jnp.int32)


def draw_regions(key, part):
    key = jax.random.fold_in(key, 11)
    row_key, col_key = jax.random.split(key)
    row_part = part_labels(row_key, H)
    col_part = part_labels(col_key, W)
    return (2 * WCOLS * row_part[:, None] + col_part[None, :]).astype(jnp.int32)


def draw_rel_index(key, part):
    key = jax.random.fold_in(key, 23)
    order = jax.random.permutation(key, (2 * WIN - 1) ** 2)
    position = jnp.arange(WIN * WIN)
    prow = position // WIN
    pcol = position % WIN
    offset = (prow[:, None] - prow[None, :] + WIN - 1) * (2 * WIN - 1) + (pcol[:, None] - pcol[None, :] + WIN - 1)
    return order[offset].astype(jnp.int32)


def draw_vectors(key, part):
    key = jax.random.fold_in(key, 37)
    gain_key, bias_key = jax.random.split(key)
    gains = jax.random.uniform(gain_key, (VEC,), jnp.float32, 0.6, 1.4)
    biases = jax.random.uniform(bias_key, (VEC,), jnp.float32, -0.6, 0.6)
    index = jnp.arange(VEC)
    is_gain = (index < D) | (index >= 5 * D) & (index < 6 * D)
    return jnp.where(is_gain, gains, biases).astype(jnp.float32)


def block_scale(rng, dims, pieces, low, largest):
    def one(dim, parts):
        steps = jax.random.uniform(jax.random.fold_in(jax.random.fold_in(rng, 6), dim), (parts,), jnp.float32, low / len(pieces), largest / len(pieces))
        return jnp.repeat(jnp.exp(steps), dims[dim] // parts).reshape((-1,) + (1,) * (len(dims) - dim - 1))

    level = one(*pieces[0])
    for cut in pieces[1:]:
        level = level * one(*cut)
    return level


def bell_draw(rng, dims, width, reach, cuts=(), kind=jnp.bfloat16):
    values = jax.random.normal(rng, dims, jnp.float32) * width
    if len(cuts) > 0:
        values = block_scale(rng, dims, cuts, -0.22, 0.18) * values
    return jnp.clip(values, min=-reach, max=reach).astype(kind)


def setup_inputs(seed: int = 0) -> dict:
    key_list = jax.random.split(jax.random.key(seed), 23)
    inputs = bell_draw(key_list[0], (IMAGES, H, W, D), 1.0, 6.0, ((0, 4), (1, 8)), jnp.float32)
    out_grad = bell_draw(key_list[1], (IMAGES, H, W, D), 1.0, 6.0, ((0, 4), (1, 8)), jnp.float32)
    regions = draw_regions(jax.random.fold_in(key_list[22], 71), 0)
    rel_index = draw_rel_index(jax.random.fold_in(key_list[22], 71), 0)
    qkv_weight = bell_draw(key_list[4], (D, 3 * D), D ** -0.5, 0.25, ((0, 4),), jnp.float32)
    qkv_first = bell_draw(key_list[5], (D, 3 * D), (0.11 * TOKENS ** 0.5), 80.0, ((0, 4),), jnp.float32)
    qkv_second = jnp.clip(jnp.exp(math.log(50.176) - 1.3862944 * jax.random.uniform(key_list[6], (D, 3 * D), jnp.float32) ** block_scale(key_list[6], (D, 3 * D), ((0, 4),), -0.2, 0.2)), 12.544, 50.176)
    proj_weight = bell_draw(key_list[7], (D, D), (D // 8) ** -0.5, 0.75, ((0, 4),), jnp.float32)
    proj_first = bell_draw(key_list[8], (D, D), (0.055 * TOKENS ** 0.5), 40.0, ((0, 4),), jnp.float32)
    proj_second = jnp.clip(jnp.exp(math.log(12.544) - 1.3862944 * jax.random.uniform(key_list[9], (D, D), jnp.float32) ** block_scale(key_list[9], (D, D), ((0, 4),), -0.2, 0.2)), 3.136, 12.544)
    up_weight = bell_draw(key_list[10], (D, FF), D ** -0.5, 0.25, ((0, 4),), jnp.float32)
    up_first = bell_draw(key_list[11], (D, FF), (0.033 * TOKENS ** 0.5), 24.0, ((0, 4),), jnp.float32)
    up_second = jnp.clip(jnp.exp(math.log(4.51584) - 1.3862944 * jax.random.uniform(key_list[12], (D, FF), jnp.float32) ** block_scale(key_list[12], (D, FF), ((0, 4),), -0.2, 0.2)), 1.12896, 4.51584)
    down_weight = bell_draw(key_list[13], (FF, D), FF ** -0.5, 0.125, ((0, 4),), jnp.float32)
    down_first = bell_draw(key_list[14], (FF, D), (0.07 * TOKENS ** 0.5), 48.0, ((0, 4),), jnp.float32)
    down_second = jnp.clip(jnp.exp(math.log(21.3248) - 1.446919 * jax.random.uniform(key_list[15], (FF, D), jnp.float32) ** block_scale(key_list[15], (FF, D), ((0, 4),), -0.2, 0.2)), 5.0176, 21.3248)
    vectors = draw_vectors(jax.random.fold_in(key_list[22], 71), 0)
    vectors_first = bell_draw(key_list[17], (VEC,), (0.1 * TOKENS ** 0.5), 64.0, (), jnp.float32)
    vectors_second = jnp.clip(jnp.exp(jax.random.uniform(key_list[18], (VEC,), jnp.float32, math.log(2.5088), math.log(50.176))), 2.5088, 50.176)
    bias_table = bell_draw(key_list[19], (HEADS, TAB), 1.0, 5.0, (), jnp.float32)
    table_first = bell_draw(key_list[20], (HEADS, TAB), (0.11 * TOKENS ** 0.5), 80.0, (), jnp.float32)
    table_second = jnp.clip(jnp.exp(jax.random.uniform(key_list[21], (HEADS, TAB), jnp.float32, math.log(12.544), math.log(50.176))), 12.544, 50.176)
    return dict(inputs=inputs, out_grad=out_grad, regions=regions, rel_index=rel_index, qkv_weight=qkv_weight, qkv_first=qkv_first, qkv_second=qkv_second, proj_weight=proj_weight, proj_first=proj_first, proj_second=proj_second, up_weight=up_weight, up_first=up_first, up_second=up_second, down_weight=down_weight, down_first=down_first, down_second=down_second, vectors=vectors, vectors_first=vectors_first, vectors_second=vectors_second, bias_table=bias_table, table_first=table_first, table_second=table_second)


@jax.custom_vjp
def low(v):
    return lax.optimization_barrier(v.astype(jnp.bfloat16)).astype(jnp.float32)

@jax.custom_vjp
def low_back(v):
    return v

def low_keep(v):
    return (low(v), None)

def low_pass(kept, grad):
    return (grad,)

def back_keep(v):
    return (v, None)

def back_low(kept, grad):
    return (low(grad),)
low.defvjp(low_keep, low_pass)
low_back.defvjp(back_keep, back_low)
norm_eps = 1e-05
mask_fill = -100.0
beta_first = 0.9
beta_second = 0.999
adam_eps = 1e-08
matrix_rate = 0.05
vector_rate = 0.3
matrix_decay = 0.05

def matmul(left, right):
    return jnp.dot(left, right, precision=lax.Precision.HIGHEST, preferred_element_type=jnp.float32)

def layer_norm(values, gain, offset):
    centred = values - lax.optimization_barrier(jnp.mean(values, axis=-1, keepdims=True))
    inverse = lax.rsqrt(lax.optimization_barrier(jnp.mean(centred * centred, axis=-1, keepdims=True)) + norm_eps)
    return centred * inverse * gain + offset

def window_split(tensor):
    rows, columns, channels = tensor.shape
    blocks = tensor.reshape(rows // WIN, WIN, columns // WIN, WIN, channels)
    return blocks.transpose(0, 2, 1, 3, 4).reshape(rows // WIN, columns // WIN, WIN * WIN, channels)

def window_join(tensor):
    row_blocks, col_blocks, positions, channels = tensor.shape
    blocks = tensor.reshape(row_blocks, col_blocks, WIN, WIN, channels)
    return blocks.transpose(0, 2, 1, 3, 4).reshape(row_blocks * WIN, col_blocks * WIN, channels)

def one_image(params, image, mask_bias):
    qkv_low, proj_low, up_low, down_low, vectors, position_bias = params
    gain_one = vectors[0:D]
    shift_one = vectors[D:2 * D]
    query_bias = vectors[2 * D:3 * D]
    value_bias = vectors[3 * D:4 * D]
    proj_bias = vectors[4 * D:5 * D]
    gain_two = vectors[5 * D:6 * D]
    shift_two = vectors[6 * D:7 * D]
    down_bias = vectors[7 * D:8 * D]
    up_bias = vectors[8 * D:8 * D + FF]
    flat_in = image.reshape(H * W, D)
    act_one = low(layer_norm(flat_in, gain_one, shift_one))
    qkv_bias = jnp.concatenate([query_bias, jnp.zeros_like(query_bias), value_bias])
    qkv_vals = low(low_back(matmul(act_one, qkv_low) + qkv_bias))
    shifted = jnp.roll(qkv_vals.reshape(H, W, 3 * D), (-SHIFT, -SHIFT), axis=(0, 1))
    windows = window_split(shifted)
    row_blocks, col_blocks = (windows.shape[0], windows.shape[1])
    queries = windows[..., 0:D].reshape(row_blocks, col_blocks, PAIRS, HEADS, HEAD_DIM)
    keys_in = windows[..., D:2 * D].reshape(row_blocks, col_blocks, PAIRS, HEADS, HEAD_DIM)
    values_in = windows[..., 2 * D:3 * D].reshape(row_blocks, col_blocks, PAIRS, HEADS, HEAD_DIM)
    raw = jnp.einsum('abihd,abjhd->abhij', queries, keys_in, precision=lax.Precision.HIGHEST)
    scores = raw * HEAD_DIM ** (-0.5) + position_bias[None, None] + mask_bias[:, :, None]
    scores = low_back(scores)
    probs = low(jax.nn.softmax(scores, axis=-1))
    attended = jnp.einsum('abhij,abjhd->abihd', probs, values_in, precision=lax.Precision.HIGHEST)
    attended = window_join(attended.reshape(row_blocks, col_blocks, PAIRS, D))
    attn = low(low_back(jnp.roll(attended, (SHIFT, SHIFT), axis=(0, 1)).reshape(H * W, D)))
    mid = flat_in + low_back(matmul(attn, proj_low) + proj_bias)
    act_two = low(layer_norm(mid, gain_two, shift_two))
    hidden = low_back(matmul(act_two, up_low) + up_bias)
    gelu_low = low(jax.nn.gelu(hidden, approximate=False))
    result = mid + low_back(matmul(gelu_low, down_low) + down_bias)
    return result.reshape(H, W, D)

def forward(mats, vectors, bias_table, inputs, regions, rel_index):
    lows = tuple((low(matrix) for matrix in mats))
    position_bias = bias_table[:, rel_index]
    labels = window_split(regions[:, :, None])[..., 0]
    mask_bias = jnp.where(labels[..., :, None] == labels[..., None, :], 0.0, mask_fill).astype(jnp.float32)
    params = lows + (vectors, position_bias)
    stepper = jax.checkpoint(one_image)

    def scan_step(carry, image):
        return (carry, stepper(params, image, mask_bias))
    return lax.scan(scan_step, None, inputs)[1]

def adam_step(param, first, second, grad, rate, decay):
    new_first = beta_first * first + (1.0 - beta_first) * grad
    new_second = beta_second * second + (1.0 - beta_second) * grad * grad
    first_hat = new_first / (1.0 - beta_first ** STEP)
    second_hat = new_second / (1.0 - beta_second ** STEP)
    new_param = param - rate * (first_hat / (jnp.sqrt(second_hat) + adam_eps) + decay * param)
    return (new_param, new_first, new_second)

def reference(inputs, out_grad, regions, rel_index, qkv_weight, qkv_first, qkv_second, proj_weight, proj_first, proj_second, up_weight, up_first, up_second, down_weight, down_first, down_second, vectors, vectors_first, vectors_second, bias_table, table_first, table_second):
    mats = (qkv_weight, proj_weight, up_weight, down_weight)

    def run(mats_in, vectors_in, table_in, inputs_in):
        return forward(mats_in, vectors_in, table_in, inputs_in, regions, rel_index)
    block_out, pull = jax.vjp(run, mats, vectors, bias_table, inputs)
    mat_grads, vector_grad, table_grad, input_grad = pull(out_grad)
    qkv_new = adam_step(qkv_weight, qkv_first, qkv_second, mat_grads[0], matrix_rate, matrix_decay)
    proj_new = adam_step(proj_weight, proj_first, proj_second, mat_grads[1], matrix_rate, matrix_decay)
    up_new = adam_step(up_weight, up_first, up_second, mat_grads[2], matrix_rate, matrix_decay)
    down_new = adam_step(down_weight, down_first, down_second, mat_grads[3], matrix_rate, matrix_decay)
    vector_new = adam_step(vectors, vectors_first, vectors_second, vector_grad, vector_rate, 0.0)
    table_new = adam_step(bias_table, table_first, table_second, table_grad, vector_rate, 0.0)
    return (block_out, input_grad, qkv_new[0], qkv_new[1], qkv_new[2], proj_new[0], proj_new[1], proj_new[2], up_new[0], up_new[1], up_new[2], down_new[0], down_new[1], down_new[2], vector_new[0], vector_new[1], vector_new[2], table_new[0], table_new[1], table_new[2])
```

```python
import jax
import jax.numpy as jnp
from jax import lax
from jax.experimental import pallas as pl
from jax.experimental.pallas import tpu as pltpu
from jax.sharding import PartitionSpec as P

HEAD_DIM = 32
WIN = 7
SHIFT = 3
STEP = 10


norm_eps = 1e-05
mask_fill = -100.0
beta_first = 0.9
beta_second = 0.999
adam_eps = 1e-08
matrix_rate = 0.05
vector_rate = 0.3
matrix_decay = 0.05
root_half = 0.7071067811865476
root_two_pi = 0.3989422804014327


def passed_along(block, axis, distance):
    devices = range(lax.axis_size(axis))
    route = [((i - distance) % len(devices), i) for i in devices]
    return lax.ppermute(block, axis, route)


def layer_norm(values, gain, offset):
    centred = values - jnp.mean(values, axis=-1, keepdims=True)
    inverse = lax.rsqrt(jnp.mean(centred * centred, axis=-1, keepdims=True) + norm_eps)
    normal = centred * inverse
    return (normal * gain + offset, normal, inverse)


def norm_back(grad_in, normal, inverse, gain):
    scaled = grad_in * gain
    centre = jnp.mean(scaled, axis=-1, keepdims=True)
    along = jnp.mean(scaled * normal, axis=-1, keepdims=True)
    return inverse * (scaled - centre - normal * along)


def to_windows(tensor):
    images, rows, columns, channels = tensor.shape
    blocks = tensor.reshape(images, rows, columns // WIN, WIN, channels)
    return blocks.transpose(0, 2, 1, 3, 4).reshape(images, columns // WIN, rows * WIN, channels)


def from_windows(tensor, rows):
    images, window_count, positions, channels = tensor.shape
    blocks = tensor.reshape(images, window_count, rows, WIN, channels)
    return blocks.transpose(0, 2, 1, 3, 4).reshape(images, rows, window_count * WIN, channels)


def split_heads(tensor, heads):
    return tensor.reshape(tensor.shape[:3] + (heads, tensor.shape[-1] // heads))


def window_scores(queries, keys_in, position_bias, mask_bias):
    raw = jnp.einsum("bwihd,bwjhd->bwhij", queries, keys_in, preferred_element_type=jnp.float32)
    return raw * HEAD_DIM ** (-0.5) + position_bias[None, None] + mask_bias[None, :, None]


def adam_step(param, first, second, grad, rate, decay):
    new_first = beta_first * first + (1.0 - beta_first) * grad
    new_second = beta_second * second + (1.0 - beta_second) * grad * grad
    first_hat = new_first / (1.0 - beta_first**STEP)
    second_hat = new_second / (1.0 - beta_second**STEP)
    new_param = param - rate * (first_hat / (jnp.sqrt(second_hat) + adam_eps) + decay * param)
    return (new_param, new_first, new_second)


def chunk_list(qkv, proj, up, down, width):
    chunks = []
    for k in range(down.shape[0] // proj.shape[0]):
        chunks.append((down, None, k))
    for k in range(up.shape[1] // width):
        chunks.append((up, k * width, 0))
    chunks.append((proj, 0, 0))
    for k in range(qkv.shape[1] // width):
        chunks.append((qkv, k * width, 0))
    return chunks


def reduce_kernel(
    qkv, proj, up, down, vec, o_qkv, o_proj, o_up, o_down, o_vec,
    from_core, to_x, from_x, to_y, from_y, mine, to_z, from_z,
    v_keep, v_core, v_x, v_y, v_z,
    core_send, core_recv, x_send, x_recv, y_send, y_recv, z_send, z_recv,
    zg_send, zg_recv, yg_send, yg_recv, v_send, v_recv,
):
    f32, bf16 = jnp.float32, jnp.bfloat16
    seq, fsdp = lax.axis_index("seq"), lax.axis_index("fsdp")
    z, y = seq // 2, seq % 2
    x, core = fsdp // 2, fsdp % 2
    sib = {"seq": seq, "fsdp": x * 2 + (1 - core)}
    across = {"seq": seq, "fsdp": (1 - x) * 2 + core}
    beside = {"seq": z * 2 + (1 - y), "fsdp": fsdp}
    others = [(z + d) % 4 for d in (1, 2, 3)]
    along = [{"seq": o * 2 + y, "fsdp": fsdp} for o in others]
    barrier = pltpu.get_barrier_semaphore()
    for dev in [sib, across, beside] + along:
        pl.semaphore_signal(barrier, inc=1, device_id=dev, device_id_type=pl.DeviceIdType.MESH)
    pl.semaphore_wait(barrier, 6)

    rows, width = o_proj.shape
    half, quarter = rows // 2, rows // 8
    ins = chunk_list(qkv, proj, up, down, width)
    outs = chunk_list(o_qkv, o_proj, o_up, o_down, width)
    count = len(ins)
    sends = []

    def send(src, dst, s_sem, r_sem, dev):
        copy = pltpu.make_async_remote_copy(
            src_ref=src, dst_ref=dst, send_sem=s_sem, recv_sem=r_sem,
            device_id=dev, device_id_type=pl.DeviceIdType.MESH,
        )
        copy.start()
        sends.append(copy)
        return copy

    def part(c, shard, off, n):
        ref, col, block = ins[c]
        if col is None:
            per = ref.shape[0] // 4
            return ref.at[pl.ds(pl.multiple_of(shard * per + block * rows + off, 16), n), :]
        return ref.at[pl.ds(pl.multiple_of(shard * rows + off, 16), n), col : col + width]

    def result(c, off, n):
        ref, col, block = outs[c]
        if col is None:
            return ref.at[pl.ds(pl.multiple_of(block * rows + off, 16), n), :]
        return ref.at[pl.ds(pl.multiple_of(off, 16), n), col : col + width]

    c_core, c_x, c_y, c_z, c_zg, c_yg = {}, {}, {}, {}, {}, {}
    vc = [send(vec, v_core, v_send.at[0], v_recv.at[0], sib)]
    for c in range(count):
        c_core[c] = [
            send(part(c, xx * 2 + (1 - core), 0, rows), from_core.at[c, xx],
                 core_send.at[c, xx], core_recv.at[c, xx], sib)
            for xx in (0, 1)
        ]

    def stage_x(c):
        for copy in c_core[c]:
            copy.wait_recv()
        total = part(c, (1 - x) * 2 + core, 0, rows)[...].astype(f32) + from_core[c, 1 - x].astype(f32)
        to_x[c] = total.astype(bf16)
        c_x[c] = send(to_x.at[c], from_x.at[c], x_send.at[c], x_recv.at[c], across)

    def three(c, off):
        here = pl.ds(pl.multiple_of(off, 16), half)
        return (
            part(c, x * 2 + core, off, half)[...].astype(f32)
            + from_core[c, x, here].astype(f32)
            + from_x[c, here].astype(f32)
        )

    def stage_y(c):
        c_x[c].wait_recv()
        to_y[c] = three(c, (1 - y) * half).astype(bf16)
        c_y[c] = send(to_y.at[c], from_y.at[c], y_send.at[c], y_recv.at[c], beside)

    def stage_z(c):
        c_y[c].wait_recv()
        total = three(c, y * half) + from_y[c].astype(f32)
        mine[c] = total
        to_z[c] = total.astype(bf16)
        c_z[c] = [
            send(to_z.at[c, pl.ds(pl.multiple_of(others[d] * quarter, 16), quarter)], from_z.at[c, d],
                 z_send.at[c, d], z_recv.at[c, d], along[d])
            for d in range(3)
        ]

    def stage_sum(c):
        for copy in c_z[c]:
            copy.wait_recv()
        total = mine[c, pl.ds(pl.multiple_of(z * quarter, 16), quarter)]
        for d in range(3):
            total = total + from_z[c, d].astype(f32)
        place = result(c, y * half + z * quarter, quarter)
        place[...] = total.astype(bf16)
        c_zg[c] = [
            send(place, place, zg_send.at[c, d], zg_recv.at[c, d], along[d]) for d in range(3)
        ]

    def stage_back(c):
        for copy in c_zg[c]:
            copy.wait_recv()
        place = result(c, y * half, half)
        c_yg[c] = send(place, place, yg_send.at[c], yg_recv.at[c], beside)

    def stage_end(c):
        c_yg[c].wait_recv()

    def vec_step(i):
        if i == 0:
            vc[0].wait_recv()
            v_keep[0] = vec[...] + v_core[...]
            vc.append(send(v_keep.at[0], v_x, v_send.at[1], v_recv.at[1], across))
        elif i == 1:
            vc[1].wait_recv()
            v_keep[1] = v_keep[0] + v_x[...]
            vc.append(send(v_keep.at[1], v_y, v_send.at[2], v_recv.at[2], beside))
        elif i == 2:
            vc[2].wait_recv()
            v_z[z] = v_keep[1] + v_y[...]
            for d in range(3):
                vc.append(send(v_z.at[z], v_z.at[z], v_send.at[3 + d], v_recv.at[3 + d], along[d]))
        elif i == 3:
            for copy in vc[3:]:
                copy.wait_recv()
            o_vec[...] = v_z[0] + v_z[1] + v_z[2] + v_z[3]

    vec_step(0)
    for c in range(count):
        stage_x(c)
    stages = [stage_y, stage_z, stage_sum, stage_back, stage_end]
    for t in range(count + len(stages) - 1):
        for s, stage in enumerate(stages):
            if 0 <= t - s < count:
                stage(t - s)
        if t in (0, 1, 2):
            vec_step(t + 1)
    for copy in sends:
        copy.wait_send()


def reduce_all(qkv, proj, up, down, vec):
    bf16 = jnp.bfloat16
    rows, width = proj.shape[0] // 4, proj.shape[1]
    n = (qkv.size + proj.size + up.size + down.size) // (4 * rows * width)
    dma = pltpu.SemaphoreType.DMA
    vmem = pl.BlockSpec(memory_space=pltpu.VMEM)
    return pl.pallas_call(
        reduce_kernel,
        out_shape=[jax.ShapeDtypeStruct((a.shape[0] // 4, a.shape[1]), bf16) for a in (qkv, proj, up, down)]
        + [jax.ShapeDtypeStruct(vec.shape, jnp.float32)],
        in_specs=[vmem] * 5,
        out_specs=[vmem] * 5,
        scratch_shapes=[
            pltpu.VMEM((n, 2, rows, width), bf16),
            pltpu.VMEM((n, rows, width), bf16),
            pltpu.VMEM((n, rows, width), bf16),
            pltpu.VMEM((n, rows // 2, width), bf16),
            pltpu.VMEM((n, rows // 2, width), bf16),
            pltpu.VMEM((n, rows // 2, width), jnp.float32),
            pltpu.VMEM((n, rows // 2, width), bf16),
            pltpu.VMEM((n, 3, rows // 8, width), bf16),
            pltpu.VMEM((2,) + vec.shape, jnp.float32),
            pltpu.VMEM(vec.shape, jnp.float32),
            pltpu.VMEM(vec.shape, jnp.float32),
            pltpu.VMEM(vec.shape, jnp.float32),
            pltpu.VMEM((4,) + vec.shape, jnp.float32),
            dma((n, 2)), dma((n, 2)), dma((n,)), dma((n,)), dma((n,)), dma((n,)),
            dma((n, 3)), dma((n, 3)), dma((n, 3)), dma((n, 3)), dma((n,)), dma((n,)),
            dma((6,)), dma((6,)),
        ],
        compiler_params=pltpu.CompilerParams(
            collective_id=0, has_side_effects=True, vmem_limit_bytes=48 * 1024 * 1024
        ),
        name="reduce_all",
    )(qkv, proj, up, down, vec)


def summed(qkv, proj, up, down, vector_grad, table_grad):
    low = [g.astype(jnp.bfloat16) for g in (qkv, proj, up, down)]
    if lax.axis_size("seq") == 8 and lax.axis_size("fsdp") == 4:
        size = vector_grad.size + table_grad.size
        padded = -(-size // 1024) * 1024
        flat = jnp.concatenate(
            [vector_grad, table_grad.reshape(-1), jnp.zeros((padded - size,), jnp.float32)]
        ).reshape(padded // 128, 128)
        *owned, total = reduce_all(*low, flat)
        total = total.reshape(-1)
        vector_sum = total[: vector_grad.size]
        table_sum = total[vector_grad.size : size].reshape(table_grad.shape)
    else:
        owned = [
            lax.psum(lax.psum_scatter(g, "fsdp", scatter_dimension=0, tiled=True), "seq") for g in low
        ]
        vector_sum, table_sum = lax.psum((vector_grad, table_grad), ("seq", "fsdp"))
    return [g.astype(jnp.float32) for g in owned], vector_sum, table_sum


def local(
    inputs,
    out_grad,
    regions,
    rel_index,
    qkv_weight,
    qkv_first,
    qkv_second,
    proj_weight,
    proj_first,
    proj_second,
    up_weight,
    up_first,
    up_second,
    down_weight,
    down_first,
    down_second,
    vectors,
    vectors_first,
    vectors_second,
    bias_table,
    table_first,
    table_second,
):
    image_count, band_rows, band_cols, model_width = inputs.shape
    hidden_width = up_weight.shape[1]
    head_count = model_width // HEAD_DIM
    window_cols = band_cols // WIN
    kept_rows = band_rows - SHIFT
    token_count = image_count * band_rows * band_cols
    gain_one = vectors[0:model_width]
    shift_one = vectors[model_width : 2 * model_width]
    query_bias = vectors[2 * model_width : 3 * model_width]
    value_bias = vectors[3 * model_width : 4 * model_width]
    proj_bias = vectors[4 * model_width : 5 * model_width]
    gain_two = vectors[5 * model_width : 6 * model_width]
    shift_two = vectors[6 * model_width : 7 * model_width]
    down_bias = vectors[7 * model_width : 8 * model_width]
    up_bias = vectors[8 * model_width : 8 * model_width + hidden_width]
    full_qkv, full_proj, full_up, full_down = (
        lax.all_gather(qkv_weight.astype(jnp.bfloat16), "fsdp", axis=0, tiled=True),
        lax.all_gather(proj_weight.astype(jnp.bfloat16), "fsdp", axis=0, tiled=True),
        lax.all_gather(up_weight.astype(jnp.bfloat16), "fsdp", axis=0, tiled=True),
        lax.all_gather(down_weight.astype(jnp.bfloat16), "fsdp", axis=0, tiled=True),
    )
    flat_in = inputs.reshape(token_count, model_width)
    normed_one, normal_one, inverse_one = layer_norm(flat_in, gain_one, shift_one)
    act_one = normed_one.astype(jnp.bfloat16)
    qkv_bias = jnp.concatenate([query_bias, jnp.zeros_like(query_bias), value_bias])
    qkv_vals = (jnp.dot(act_one, full_qkv, preferred_element_type=jnp.float32) + qkv_bias).astype(
        jnp.bfloat16
    )
    qkv_band = qkv_vals.reshape(image_count, band_rows, band_cols, 3 * model_width)
    below = passed_along(qkv_band[:, :SHIFT], "seq", -1)
    qkv_windows = to_windows(
        jnp.roll(jnp.concatenate([qkv_band[:, SHIFT:], below], axis=1), -SHIFT, axis=2)
    )
    queries = split_heads(qkv_windows[..., 0:model_width], head_count)
    keys_in = split_heads(qkv_windows[..., model_width : 2 * model_width], head_count)
    values_in = split_heads(qkv_windows[..., 2 * model_width : 3 * model_width], head_count)
    pairs = rel_index.shape[0]
    table_size = bias_table.shape[1]
    one_hot = (
        rel_index.reshape(-1)[:, None] == jnp.arange(table_size, dtype=jnp.int32)[None, :]
    ).astype(jnp.float32)
    position_bias = jnp.dot(bias_table, one_hot.T, precision=lax.Precision.HIGHEST).reshape(
        head_count, pairs, pairs
    )
    labels = (
        regions.reshape(band_rows, window_cols, WIN).transpose(1, 0, 2).reshape(window_cols, pairs)
    )
    mask_bias = jnp.where(labels[:, :, None] == labels[:, None, :], 0.0, mask_fill).astype(
        jnp.float32
    )
    scores = window_scores(queries, keys_in, position_bias, mask_bias)
    peak = jnp.max(scores, axis=-1, keepdims=True)
    log_total = peak + jnp.log(jnp.sum(jnp.exp(scores - peak), axis=-1, keepdims=True))
    probs_low = jnp.exp(scores - log_total).astype(jnp.bfloat16)
    attended = jnp.einsum(
        "bwhij,bwjhd->bwihd", probs_low, values_in, preferred_element_type=jnp.float32
    )
    attended_low = attended.astype(jnp.bfloat16).reshape(
        image_count, window_cols, pairs, model_width
    )
    attn_band = jnp.roll(from_windows(attended_low, band_rows), SHIFT, axis=2)
    above = passed_along(attn_band[:, kept_rows:], "seq", 1)
    attn_own = jnp.concatenate([above, attn_band[:, :kept_rows]], axis=1).reshape(
        token_count, model_width
    )
    mid = flat_in + (jnp.dot(attn_own, full_proj, preferred_element_type=jnp.float32) + proj_bias)
    normed_two, normal_two, inverse_two = layer_norm(mid, gain_two, shift_two)
    act_two = normed_two.astype(jnp.bfloat16)
    hidden = jnp.dot(act_two, full_up, preferred_element_type=jnp.float32) + up_bias
    gelu_low = jax.nn.gelu(hidden, approximate=False).astype(jnp.bfloat16)
    block_out = mid + (jnp.dot(gelu_low, full_down, preferred_element_type=jnp.float32) + down_bias)
    grad_flat = out_grad.reshape(token_count, model_width)
    grad_low = grad_flat.astype(jnp.bfloat16)
    down_grad = jnp.dot(gelu_low.T, grad_low, preferred_element_type=jnp.float32)
    down_bias_grad = jnp.sum(grad_low.astype(jnp.float32), axis=0)
    slope = (
        0.5 * (1.0 + lax.erf(hidden * root_half))
        + hidden * jnp.exp(-0.5 * hidden * hidden) * root_two_pi
    )
    hidden_grad = (
        jnp.dot(grad_low, full_down.T, preferred_element_type=jnp.float32) * slope
    ).astype(jnp.bfloat16)
    up_grad = jnp.dot(act_two.T, hidden_grad, preferred_element_type=jnp.float32)
    up_bias_grad = jnp.sum(hidden_grad.astype(jnp.float32), axis=0)
    act_two_grad = jnp.dot(hidden_grad, full_up.T, preferred_element_type=jnp.float32)
    gain_two_grad = jnp.sum(act_two_grad * normal_two, axis=0)
    shift_two_grad = jnp.sum(act_two_grad, axis=0)
    mid_grad = grad_flat + norm_back(act_two_grad, normal_two, inverse_two, gain_two)
    mid_low = mid_grad.astype(jnp.bfloat16)
    proj_grad = jnp.dot(attn_own.T, mid_low, preferred_element_type=jnp.float32)
    proj_bias_grad = jnp.sum(mid_low.astype(jnp.float32), axis=0)
    attn_grad = jnp.dot(mid_low, full_proj.T, preferred_element_type=jnp.float32).astype(
        jnp.bfloat16
    )
    attn_grad = attn_grad.reshape(image_count, band_rows, band_cols, model_width)
    below_grad = passed_along(attn_grad[:, :SHIFT], "seq", -1)
    grad_windows = to_windows(
        jnp.roll(jnp.concatenate([attn_grad[:, SHIFT:], below_grad], axis=1), -SHIFT, axis=2)
    )
    grad_heads = split_heads(grad_windows, head_count)
    scores_again = window_scores(queries, keys_in, position_bias, mask_bias)
    probs = jnp.exp(scores_again - log_total)
    probs_again = probs.astype(jnp.bfloat16)
    value_grad = jnp.einsum(
        "bwhij,bwihd->bwjhd", probs_again, grad_heads, preferred_element_type=jnp.float32
    )
    prob_grad = jnp.einsum(
        "bwihd,bwjhd->bwhij", grad_heads, values_in, preferred_element_type=jnp.float32
    )
    score_grad = (probs * (prob_grad - jnp.sum(probs * prob_grad, axis=-1, keepdims=True))).astype(
        jnp.bfloat16
    )
    score_total = jnp.sum(score_grad.astype(jnp.float32), axis=(0, 1)).reshape(
        head_count, pairs * pairs
    )
    table_grad = jnp.dot(score_total, one_hot, precision=lax.Precision.HIGHEST)
    query_grad = jnp.einsum(
        "bwhij,bwjhd->bwihd", score_grad, keys_in, preferred_element_type=jnp.float32
    ) * HEAD_DIM ** (-0.5)
    key_grad = jnp.einsum(
        "bwhij,bwihd->bwjhd", score_grad, queries, preferred_element_type=jnp.float32
    ) * HEAD_DIM ** (-0.5)
    flat_shape = (image_count, window_cols, pairs, model_width)
    stacked = jnp.concatenate(
        [
            query_grad.reshape(flat_shape),
            key_grad.reshape(flat_shape),
            value_grad.reshape(flat_shape),
        ],
        axis=-1,
    ).astype(jnp.bfloat16)
    qkv_grad_band = jnp.roll(from_windows(stacked, band_rows), SHIFT, axis=2)
    above_grad = passed_along(qkv_grad_band[:, kept_rows:], "seq", 1)
    qkv_grad = jnp.concatenate([above_grad, qkv_grad_band[:, :kept_rows]], axis=1).reshape(
        token_count, 3 * model_width
    )
    qkv_weight_grad = jnp.dot(act_one.T, qkv_grad, preferred_element_type=jnp.float32)
    bias_sums = jnp.sum(qkv_grad.astype(jnp.float32), axis=0)
    act_one_grad = jnp.dot(qkv_grad, full_qkv.T, preferred_element_type=jnp.float32)
    gain_one_grad = jnp.sum(act_one_grad * normal_one, axis=0)
    shift_one_grad = jnp.sum(act_one_grad, axis=0)
    input_grad = mid_grad + norm_back(act_one_grad, normal_one, inverse_one, gain_one)
    vector_grad = jnp.concatenate(
        [
            gain_one_grad,
            shift_one_grad,
            bias_sums[0:model_width],
            bias_sums[2 * model_width : 3 * model_width],
            proj_bias_grad,
            gain_two_grad,
            shift_two_grad,
            down_bias_grad,
            up_bias_grad,
        ]
    )
    reduced, vector_sum, table_sum = summed(
        qkv_weight_grad, proj_grad, up_grad, down_grad, vector_grad, table_grad
    )
    qkv_new = adam_step(qkv_weight, qkv_first, qkv_second, reduced[0], matrix_rate, matrix_decay)
    proj_new = adam_step(
        proj_weight, proj_first, proj_second, reduced[1], matrix_rate, matrix_decay
    )
    up_new = adam_step(up_weight, up_first, up_second, reduced[2], matrix_rate, matrix_decay)
    down_new = adam_step(
        down_weight, down_first, down_second, reduced[3], matrix_rate, matrix_decay
    )
    vector_new = adam_step(vectors, vectors_first, vectors_second, vector_sum, vector_rate, 0.0)
    table_new = adam_step(bias_table, table_first, table_second, table_sum, vector_rate, 0.0)
    return (
        block_out.reshape(inputs.shape),
        input_grad.reshape(inputs.shape),
        qkv_new[0],
        qkv_new[1],
        qkv_new[2],
        proj_new[0],
        proj_new[1],
        proj_new[2],
        up_new[0],
        up_new[1],
        up_new[2],
        down_new[0],
        down_new[1],
        down_new[2],
        vector_new[0],
        vector_new[1],
        vector_new[2],
        table_new[0],
        table_new[1],
        table_new[2],
    )


def solution(mesh):
    placed = (
        P("fsdp", "seq", None, None),
        P("fsdp", "seq", None, None),
        P("seq", None),
        P(),
        P("fsdp", None),
        P("fsdp", None),
        P("fsdp", None),
        P("fsdp", None),
        P("fsdp", None),
        P("fsdp", None),
        P("fsdp", None),
        P("fsdp", None),
        P("fsdp", None),
        P("fsdp", None),
        P("fsdp", None),
        P("fsdp", None),
        P(),
        P(),
        P(),
        P(),
        P(),
        P(),
    )
    return jax.shard_map(
        local,
        mesh=mesh,
        in_specs=placed,
        out_specs=(
            P("fsdp", "seq", None, None),
            P("fsdp", "seq", None, None),
            P("fsdp", None),
            P("fsdp", None),
            P("fsdp", None),
            P("fsdp", None),
            P("fsdp", None),
            P("fsdp", None),
            P("fsdp", None),
            P("fsdp", None),
            P("fsdp", None),
            P("fsdp", None),
            P("fsdp", None),
            P("fsdp", None),
            P(),
            P(),
            P(),
            P(),
            P(),
            P(),
        ),
        check_vma=False,
    )
```

```python
import jax
import jax.numpy as jnp
import numpy as np
from jax import lax
from jax.experimental import pallas as pl
from jax.experimental.pallas import tpu as pltpu
from jax.sharding import PartitionSpec as P

HEAD_DIM = 32
WIN = 7
SHIFT = 3
STEP = 10


norm_eps = 1e-05
mask_fill = -100.0
beta_first = 0.9
beta_second = 0.999
adam_eps = 1e-08
matrix_rate = 0.05
vector_rate = 0.3
matrix_decay = 0.05
root_half = 0.7071067811865476
root_two_pi = 0.3989422804014327


def passed_along(block, axis, distance):
    devices = range(lax.axis_size(axis))
    route = [((i - distance) % len(devices), i) for i in devices]
    return lax.ppermute(block, axis, route)


def layer_norm(values, gain, offset):
    centred = values - jnp.mean(values, axis=-1, keepdims=True)
    inverse = lax.rsqrt(jnp.mean(centred * centred, axis=-1, keepdims=True) + norm_eps)
    normal = centred * inverse
    return (normal * gain + offset, normal, inverse)


def norm_back(grad_in, normal, inverse, gain):
    scaled = grad_in * gain
    centre = jnp.mean(scaled, axis=-1, keepdims=True)
    along = jnp.mean(scaled * normal, axis=-1, keepdims=True)
    return inverse * (scaled - centre - normal * along)


def adam_step(param, first, second, grad, rate, decay):
    new_first = beta_first * first + (1.0 - beta_first) * grad
    new_second = beta_second * second + (1.0 - beta_second) * grad * grad
    first_hat = new_first / (1.0 - beta_first**STEP)
    second_hat = new_second / (1.0 - beta_second**STEP)
    new_param = param - rate * (first_hat / (jnp.sqrt(second_hat) + adam_eps) + decay * param)
    return (new_param, new_first, new_second)


def chunk_list(qkv, proj, up, down, width):
    chunks = []
    for k in range(down.shape[0] // proj.shape[0]):
        chunks.append((down, None, k))
    for k in range(up.shape[1] // width):
        chunks.append((up, k * width, 0))
    chunks.append((proj, 0, 0))
    for k in range(qkv.shape[1] // width):
        chunks.append((qkv, k * width, 0))
    return chunks


def reduce_kernel(
    qkv, proj, up, down, vec, o_qkv, o_proj, o_up, o_down, o_vec,
    from_core, to_x, from_x, to_y, from_y, mine, to_z, from_z,
    v_keep, v_core, v_x, v_y, v_z,
    core_send, core_recv, x_send, x_recv, y_send, y_recv, z_send, z_recv,
    zg_send, zg_recv, yg_send, yg_recv, v_send, v_recv,
):
    f32, bf16 = jnp.float32, jnp.bfloat16
    seq, fsdp = lax.axis_index("seq"), lax.axis_index("fsdp")
    z, y = seq // 2, seq % 2
    x, core = fsdp // 2, fsdp % 2
    sib = {"seq": seq, "fsdp": x * 2 + (1 - core)}
    across = {"seq": seq, "fsdp": (1 - x) * 2 + core}
    beside = {"seq": z * 2 + (1 - y), "fsdp": fsdp}
    others = [(z + d) % 4 for d in (1, 2, 3)]
    along = [{"seq": o * 2 + y, "fsdp": fsdp} for o in others]
    barrier = pltpu.get_barrier_semaphore()
    for dev in [sib, across, beside] + along:
        pl.semaphore_signal(barrier, inc=1, device_id=dev, device_id_type=pl.DeviceIdType.MESH)
    pl.semaphore_wait(barrier, 6)

    rows, width = o_proj.shape
    half, quarter = rows // 2, rows // 8
    ins = chunk_list(qkv, proj, up, down, width)
    outs = chunk_list(o_qkv, o_proj, o_up, o_down, width)
    count = len(ins)
    sends = []

    def send(src, dst, s_sem, r_sem, dev):
        copy = pltpu.make_async_remote_copy(
            src_ref=src, dst_ref=dst, send_sem=s_sem, recv_sem=r_sem,
            device_id=dev, device_id_type=pl.DeviceIdType.MESH,
        )
        copy.start()
        sends.append(copy)
        return copy

    def part(c, shard, off, n):
        ref, col, block = ins[c]
        if col is None:
            per = ref.shape[0] // 4
            return ref.at[pl.ds(pl.multiple_of(shard * per + block * rows + off, 16), n), :]
        return ref.at[pl.ds(pl.multiple_of(shard * rows + off, 16), n), col : col + width]

    def result(c, off, n):
        ref, col, block = outs[c]
        if col is None:
            return ref.at[pl.ds(pl.multiple_of(block * rows + off, 16), n), :]
        return ref.at[pl.ds(pl.multiple_of(off, 16), n), col : col + width]

    c_core, c_x, c_y, c_z, c_zg, c_yg = {}, {}, {}, {}, {}, {}
    vc = [send(vec, v_core, v_send.at[0], v_recv.at[0], sib)]
    for c in range(count):
        c_core[c] = [
            send(part(c, xx * 2 + (1 - core), 0, rows), from_core.at[c, xx],
                 core_send.at[c, xx], core_recv.at[c, xx], sib)
            for xx in (0, 1)
        ]

    def stage_x(c):
        for copy in c_core[c]:
            copy.wait_recv()
        total = part(c, (1 - x) * 2 + core, 0, rows)[...].astype(f32) + from_core[c, 1 - x].astype(f32)
        to_x[c] = total.astype(bf16)
        c_x[c] = send(to_x.at[c], from_x.at[c], x_send.at[c], x_recv.at[c], across)

    def three(c, off):
        here = pl.ds(pl.multiple_of(off, 16), half)
        return (
            part(c, x * 2 + core, off, half)[...].astype(f32)
            + from_core[c, x, here].astype(f32)
            + from_x[c, here].astype(f32)
        )

    def stage_y(c):
        c_x[c].wait_recv()
        to_y[c] = three(c, (1 - y) * half).astype(bf16)
        c_y[c] = send(to_y.at[c], from_y.at[c], y_send.at[c], y_recv.at[c], beside)

    def stage_z(c):
        c_y[c].wait_recv()
        total = three(c, y * half) + from_y[c].astype(f32)
        mine[c] = total
        to_z[c] = total.astype(bf16)
        c_z[c] = [
            send(to_z.at[c, pl.ds(pl.multiple_of(others[d] * quarter, 16), quarter)], from_z.at[c, d],
                 z_send.at[c, d], z_recv.at[c, d], along[d])
            for d in range(3)
        ]

    def stage_sum(c):
        for copy in c_z[c]:
            copy.wait_recv()
        total = mine[c, pl.ds(pl.multiple_of(z * quarter, 16), quarter)]
        for d in range(3):
            total = total + from_z[c, d].astype(f32)
        place = result(c, y * half + z * quarter, quarter)
        place[...] = total.astype(bf16)
        c_zg[c] = [
            send(place, place, zg_send.at[c, d], zg_recv.at[c, d], along[d]) for d in range(3)
        ]

    def stage_back(c):
        for copy in c_zg[c]:
            copy.wait_recv()
        place = result(c, y * half, half)
        c_yg[c] = send(place, place, yg_send.at[c], yg_recv.at[c], beside)

    def stage_end(c):
        c_yg[c].wait_recv()

    def vec_step(i):
        if i == 0:
            vc[0].wait_recv()
            v_keep[0] = vec[...] + v_core[...]
            vc.append(send(v_keep.at[0], v_x, v_send.at[1], v_recv.at[1], across))
        elif i == 1:
            vc[1].wait_recv()
            v_keep[1] = v_keep[0] + v_x[...]
            vc.append(send(v_keep.at[1], v_y, v_send.at[2], v_recv.at[2], beside))
        elif i == 2:
            vc[2].wait_recv()
            v_z[z] = v_keep[1] + v_y[...]
            for d in range(3):
                vc.append(send(v_z.at[z], v_z.at[z], v_send.at[3 + d], v_recv.at[3 + d], along[d]))
        elif i == 3:
            for copy in vc[3:]:
                copy.wait_recv()
            o_vec[...] = v_z[0] + v_z[1] + v_z[2] + v_z[3]

    vec_step(0)
    for c in range(count):
        stage_x(c)
    stages = [stage_y, stage_z, stage_sum, stage_back, stage_end]
    for t in range(count + len(stages) - 1):
        for s, stage in enumerate(stages):
            if 0 <= t - s < count:
                stage(t - s)
        if t in (0, 1, 2):
            vec_step(t + 1)
    for copy in sends:
        copy.wait_send()


def reduce_all(qkv, proj, up, down, vec):
    bf16 = jnp.bfloat16
    rows, width = proj.shape[0] // 4, proj.shape[1]
    n = (qkv.size + proj.size + up.size + down.size) // (4 * rows * width)
    dma = pltpu.SemaphoreType.DMA
    vmem = pl.BlockSpec(memory_space=pltpu.VMEM)
    return pl.pallas_call(
        reduce_kernel,
        out_shape=[jax.ShapeDtypeStruct((a.shape[0] // 4, a.shape[1]), bf16) for a in (qkv, proj, up, down)]
        + [jax.ShapeDtypeStruct(vec.shape, jnp.float32)],
        in_specs=[vmem] * 5,
        out_specs=[vmem] * 5,
        scratch_shapes=[
            pltpu.VMEM((n, 2, rows, width), bf16),
            pltpu.VMEM((n, rows, width), bf16),
            pltpu.VMEM((n, rows, width), bf16),
            pltpu.VMEM((n, rows // 2, width), bf16),
            pltpu.VMEM((n, rows // 2, width), bf16),
            pltpu.VMEM((n, rows // 2, width), jnp.float32),
            pltpu.VMEM((n, rows // 2, width), bf16),
            pltpu.VMEM((n, 3, rows // 8, width), bf16),
            pltpu.VMEM((2,) + vec.shape, jnp.float32),
            pltpu.VMEM(vec.shape, jnp.float32),
            pltpu.VMEM(vec.shape, jnp.float32),
            pltpu.VMEM(vec.shape, jnp.float32),
            pltpu.VMEM((4,) + vec.shape, jnp.float32),
            dma((n, 2)), dma((n, 2)), dma((n,)), dma((n,)), dma((n,)), dma((n,)),
            dma((n, 3)), dma((n, 3)), dma((n, 3)), dma((n, 3)), dma((n,)), dma((n,)),
            dma((6,)), dma((6,)),
        ],
        compiler_params=pltpu.CompilerParams(
            collective_id=0, has_side_effects=True, vmem_limit_bytes=48 * 1024 * 1024
        ),
        name="reduce_all",
    )(qkv, proj, up, down, vec)


def summed(qkv, proj, up, down, vector_grad, table_grad):
    low = [g.astype(jnp.bfloat16) for g in (qkv, proj, up, down)]
    if lax.axis_size("seq") == 8 and lax.axis_size("fsdp") == 4:
        size = vector_grad.size + table_grad.size
        padded = -(-size // 1024) * 1024
        flat = jnp.concatenate(
            [vector_grad, table_grad.reshape(-1), jnp.zeros((padded - size,), jnp.float32)]
        ).reshape(padded // 128, 128)
        *owned, total = reduce_all(*low, flat)
        total = total.reshape(-1)
        vector_sum = total[: vector_grad.size]
        table_sum = total[vector_grad.size : size].reshape(table_grad.shape)
    else:
        owned = [
            lax.psum(lax.psum_scatter(g, "fsdp", scatter_dimension=0, tiled=True), "seq") for g in low
        ]
        vector_sum, table_sum = lax.psum((vector_grad, table_grad), ("seq", "fsdp"))
    return [g.astype(jnp.float32) for g in owned], vector_sum, table_sum


SPAN = 64
GROUP = 256


def gather_kernel(qkv, proj, o_qkv, o_proj, sib_send, sib_recv, x_send, x_recv, on_send, on_recv):
    seq, fsdp = lax.axis_index("seq"), lax.axis_index("fsdp")
    x, core = fsdp // 2, fsdp % 2
    sib = {"seq": seq, "fsdp": x * 2 + (1 - core)}
    away = (1 - x) * 2 + core
    across = {"seq": seq, "fsdp": away}
    barrier = pltpu.get_barrier_semaphore()
    for dev in (sib, across):
        pl.semaphore_signal(barrier, inc=1, device_id=dev, device_id_type=pl.DeviceIdType.MESH)
    rows, width = proj.shape
    places = [(o_qkv, k * width) for k in range(qkv.shape[1] // width)] + [(o_proj, 0)]
    own = pl.ds(pl.multiple_of(fsdp * rows, 16), rows)
    o_qkv[own, :] = qkv[...].astype(jnp.bfloat16)
    o_proj[own, :] = proj[...].astype(jnp.bfloat16)
    pl.semaphore_wait(barrier, 2)
    sends = []

    def send(i, shard, s_sem, r_sem, dev):
        ref, col = places[i]
        place = ref.at[pl.ds(pl.multiple_of(shard * rows, 16), rows), col : col + width]
        copy = pltpu.make_async_remote_copy(
            src_ref=place, dst_ref=place, send_sem=s_sem.at[i], recv_sem=r_sem.at[i],
            device_id=dev, device_id_type=pl.DeviceIdType.MESH,
        )
        copy.start()
        sends.append(copy)
        return copy

    count = len(places)
    first = [send(i, fsdp, x_send, x_recv, across) for i in range(count)]
    near = [send(i, fsdp, sib_send, sib_recv, sib) for i in range(count)]
    far = []
    for i in range(count):
        first[i].wait_recv()
        far.append(send(i, away, on_send, on_recv, sib))
    for copy in near + far:
        copy.wait_recv()
    for copy in sends:
        copy.wait_send()


def gather_first(qkv, proj):
    count = qkv.shape[1] // proj.shape[1] + 1
    vmem = pl.BlockSpec(memory_space=pltpu.VMEM)
    dma = pltpu.SemaphoreType.DMA
    return pl.pallas_call(
        gather_kernel,
        out_shape=[jax.ShapeDtypeStruct((4 * a.shape[0], a.shape[1]), jnp.bfloat16) for a in (qkv, proj)],
        in_specs=[vmem] * 2,
        out_specs=[vmem] * 2,
        scratch_shapes=[dma((count,))] * 6,
        compiler_params=pltpu.CompilerParams(
            collective_id=1, has_side_effects=True, vmem_limit_bytes=16 * 1024 * 1024
        ),
        name="gather_first",
    )(qkv, proj)


def head_masks():
    lane = lax.broadcasted_iota(jnp.int32, (SPAN, GROUP), 1) // HEAD_DIM
    return [lane == h for h in range(GROUP // HEAD_DIM)]


def spread(block, masks):
    return jnp.concatenate([jnp.where(m, block, jnp.zeros_like(block)) for m in masks], axis=0)


def merged(tall, masks):
    total = jnp.zeros((SPAN, GROUP), jnp.float32)
    for h, m in enumerate(masks):
        total = total + jnp.where(m, tall[h * SPAN : (h + 1) * SPAN], 0.0)
    return total


def dot_f32(a, b, dims=((1,), (0,))):
    return lax.dot_general(a, b, (dims, ((), ())), preferred_element_type=jnp.float32)


def attend_kernel(qkv, take, give, bias, mask, out, probs, q_w, k_w, v_w, o_w):
    bf16 = jnp.bfloat16
    width = out.shape[1]
    cols = mask.shape[0]
    windows = take.shape[0] // SPAN
    heads = GROUP // HEAD_DIM
    tall = heads * SPAN
    pad_key = lax.broadcasted_iota(jnp.int32, (1, SPAN), 1) >= WIN * WIN
    masks = head_masks()
    for g in range(width // GROUP):
        for i, ref in enumerate((q_w, k_w, v_w)):
            start = i * width + g * GROUP
            ref[...] = dot_f32(take[...], qkv[:, start : start + GROUP]).astype(bf16)
        shift = jnp.where(pad_key, -1e30, bias[g * tall : (g + 1) * tall, :])

        for n in range(windows):
            here = pl.ds(n * SPAN, SPAN)
            tall_q = spread(q_w[here, :], masks)
            scores = dot_f32(tall_q, k_w[here, :], ((1,), (1,))) * HEAD_DIM ** (-0.5) + shift
            scores = (scores.reshape(heads, SPAN, SPAN) + mask[n % cols][None]).reshape(tall, SPAN)
            grown = jnp.exp(scores - jnp.max(scores, axis=-1, keepdims=True))
            low = (grown / jnp.sum(grown, axis=-1, keepdims=True)).astype(bf16)
            probs[g * windows + n] = low
            o_w[here, :] = merged(dot_f32(low, v_w[here, :]), masks).astype(bf16)
        out[:, g * GROUP : (g + 1) * GROUP] = dot_f32(give[...], o_w[...]).astype(bf16)


def attend_back_kernel(qkv, grad, take, give, probs, out, table, q_w, k_w, v_w, d_w, gq_w, gk_w, gv_w):
    bf16 = jnp.bfloat16
    width = grad.shape[1]
    windows = take.shape[0] // SPAN
    heads = GROUP // HEAD_DIM
    tall = heads * SPAN
    scale = HEAD_DIM ** (-0.5)
    masks = head_masks()
    for g in range(width // GROUP):
        for i, ref in enumerate((q_w, k_w, v_w)):
            start = i * width + g * GROUP
            ref[...] = dot_f32(take[...], qkv[:, start : start + GROUP]).astype(bf16)
        d_w[...] = dot_f32(take[...], grad[:, g * GROUP : (g + 1) * GROUP]).astype(bf16)
        total = jnp.zeros((tall, SPAN), jnp.float32)
        for n in range(windows):
            here = pl.ds(n * SPAN, SPAN)
            tall_q = spread(q_w[here, :], masks)
            tall_d = spread(d_w[here, :], masks)
            low = probs[g * windows + n]
            prob = low.astype(jnp.float32)
            gv_w[here, :] = dot_f32(low, tall_d, ((0,), (0,))).astype(bf16)
            prob_grad = dot_f32(tall_d, v_w[here, :], ((1,), (1,)))
            along = jnp.sum(prob * prob_grad, axis=-1, keepdims=True)
            score_low = (prob * (prob_grad - along)).astype(bf16)
            total = total + score_low.astype(jnp.float32)
            gq_w[here, :] = (merged(dot_f32(score_low, k_w[here, :]), masks) * scale).astype(bf16)
            gk_w[here, :] = (dot_f32(score_low, tall_q, ((0,), (0,))) * scale).astype(bf16)
        table[g * tall : (g + 1) * tall, :] = total
        for i, ref in enumerate((gq_w, gk_w, gv_w)):
            start = i * width + g * GROUP
            out[:, start : start + GROUP] = dot_f32(give[...], ref[...]).astype(bf16)


def window_places(rows, cols, images):
    place = np.zeros((images * (cols // WIN) * SPAN, rows * cols * images), np.float32)
    for image in range(images):
        for w in range(cols // WIN):
            for r in range(rows):
                for c in range(WIN):
                    token = (r * cols + (w * WIN + c + SHIFT) % cols) * images + image
                    place[(image * (cols // WIN) + w) * SPAN + r * WIN + c, token] = 1.0
    return jnp.asarray(place, jnp.bfloat16)


def attend(qkv, take, give, bias, mask):
    tokens, width = qkv.shape[0], qkv.shape[1] // 3
    groups, windows = width // GROUP, take.shape[0] // SPAN
    tall = GROUP // HEAD_DIM * SPAN
    vmem = pl.BlockSpec(memory_space=pltpu.VMEM)
    return pl.pallas_call(
        attend_kernel,
        out_shape=[
            jax.ShapeDtypeStruct((tokens, width), jnp.bfloat16),
            jax.ShapeDtypeStruct((groups * windows, tall, SPAN), jnp.bfloat16),
        ],
        in_specs=[vmem] * 5,
        out_specs=[vmem] * 2,
        scratch_shapes=[pltpu.VMEM((take.shape[0], GROUP), jnp.bfloat16)] * 4,
        compiler_params=pltpu.CompilerParams(vmem_limit_bytes=32 * 1024 * 1024),
        name="attend",
    )(qkv, take, give, bias, mask)


def attend_back(qkv, grad, take, give, probs):
    tall = GROUP // HEAD_DIM * SPAN
    vmem = pl.BlockSpec(memory_space=pltpu.VMEM)
    return pl.pallas_call(
        attend_back_kernel,
        out_shape=[
            jax.ShapeDtypeStruct(qkv.shape, jnp.bfloat16),
            jax.ShapeDtypeStruct((grad.shape[1] // GROUP * tall, SPAN), jnp.float32),
        ],
        in_specs=[vmem] * 5,
        out_specs=[vmem] * 2,
        scratch_shapes=[pltpu.VMEM((take.shape[0], GROUP), jnp.bfloat16)] * 7,
        compiler_params=pltpu.CompilerParams(vmem_limit_bytes=32 * 1024 * 1024),
        name="attend_back",
    )(qkv, grad, take, give, probs)


def local(
    inputs,
    out_grad,
    regions,
    rel_index,
    qkv_weight,
    qkv_first,
    qkv_second,
    proj_weight,
    proj_first,
    proj_second,
    up_weight,
    up_first,
    up_second,
    down_weight,
    down_first,
    down_second,
    vectors,
    vectors_first,
    vectors_second,
    bias_table,
    table_first,
    table_second,
):
    image_count, band_rows, band_cols, model_width = inputs.shape
    hidden_width = up_weight.shape[1]
    head_count = model_width // HEAD_DIM
    window_cols = band_cols // WIN
    token_count = image_count * band_rows * band_cols
    gain_one = vectors[0:model_width]
    shift_one = vectors[model_width : 2 * model_width]
    query_bias = vectors[2 * model_width : 3 * model_width]
    value_bias = vectors[3 * model_width : 4 * model_width]
    proj_bias = vectors[4 * model_width : 5 * model_width]
    gain_two = vectors[5 * model_width : 6 * model_width]
    shift_two = vectors[6 * model_width : 7 * model_width]
    down_bias = vectors[7 * model_width : 8 * model_width]
    up_bias = vectors[8 * model_width : 8 * model_width + hidden_width]
    if lax.axis_size("seq") == 8 and lax.axis_size("fsdp") == 4:
        full_qkv, full_proj = gather_first(qkv_weight, proj_weight)
    else:
        full_qkv = lax.all_gather(qkv_weight.astype(jnp.bfloat16), "fsdp", axis=0, tiled=True)
        full_proj = lax.all_gather(proj_weight.astype(jnp.bfloat16), "fsdp", axis=0, tiled=True)
    full_up = lax.all_gather(up_weight.astype(jnp.bfloat16), "fsdp", axis=0, tiled=True)
    full_down = lax.all_gather(down_weight.astype(jnp.bfloat16), "fsdp", axis=0, tiled=True)
    sent = SHIFT * band_cols * image_count
    kept = token_count - sent
    flat_in = inputs.transpose(1, 2, 0, 3).reshape(token_count, model_width)
    normed_one, normal_one, inverse_one = layer_norm(flat_in, gain_one, shift_one)
    act_one = normed_one.astype(jnp.bfloat16)
    qkv_bias = jnp.concatenate([query_bias, jnp.zeros_like(query_bias), value_bias])
    qkv_vals = (jnp.dot(act_one, full_qkv, preferred_element_type=jnp.float32) + qkv_bias).astype(
        jnp.bfloat16
    )
    below = passed_along(qkv_vals[:sent], "seq", -1)
    qkv_ext = jnp.concatenate([qkv_vals[sent:], below], axis=0)
    pairs = rel_index.shape[0]
    table_size = bias_table.shape[1]
    rel_padded = jnp.pad(rel_index, ((0, SPAN - pairs), (0, SPAN - pairs)), constant_values=-1)
    one_hot = (
        rel_padded.reshape(-1)[:, None] == jnp.arange(table_size, dtype=jnp.int32)[None, :]
    ).astype(jnp.float32)
    position_bias = jnp.dot(bias_table, one_hot.T, precision=lax.Precision.HIGHEST).reshape(
        head_count * SPAN, SPAN
    )
    labels = (
        regions.reshape(band_rows, window_cols, WIN).transpose(1, 0, 2).reshape(window_cols, pairs)
    )
    labels = jnp.pad(labels, ((0, 0), (0, SPAN - pairs)), constant_values=-1)
    mask_bias = jnp.where(labels[:, :, None] == labels[:, None, :], 0.0, mask_fill).astype(
        jnp.float32
    )
    take = window_places(band_rows, band_cols, image_count)
    give = take.T
    attended, probs_low = attend(qkv_ext, take, give, position_bias, mask_bias)
    above = passed_along(attended[kept:], "seq", 1)
    attn_own = jnp.concatenate([above, attended[:kept]], axis=0)
    mid = flat_in + (jnp.dot(attn_own, full_proj, preferred_element_type=jnp.float32) + proj_bias)
    normed_two, normal_two, inverse_two = layer_norm(mid, gain_two, shift_two)
    act_two = normed_two.astype(jnp.bfloat16)
    hidden = jnp.dot(act_two, full_up, preferred_element_type=jnp.float32) + up_bias
    gelu_low = jax.nn.gelu(hidden, approximate=False).astype(jnp.bfloat16)
    block_out = mid + (jnp.dot(gelu_low, full_down, preferred_element_type=jnp.float32) + down_bias)
    grad_flat = out_grad.transpose(1, 2, 0, 3).reshape(token_count, model_width)
    grad_low = grad_flat.astype(jnp.bfloat16)
    down_grad = jnp.dot(gelu_low.T, grad_low, preferred_element_type=jnp.float32)
    down_bias_grad = jnp.sum(grad_low.astype(jnp.float32), axis=0)
    slope = (
        0.5 * (1.0 + lax.erf(hidden * root_half))
        + hidden * jnp.exp(-0.5 * hidden * hidden) * root_two_pi
    )
    hidden_grad = (
        jnp.dot(grad_low, full_down.T, preferred_element_type=jnp.float32) * slope
    ).astype(jnp.bfloat16)
    up_grad = jnp.dot(act_two.T, hidden_grad, preferred_element_type=jnp.float32)
    up_bias_grad = jnp.sum(hidden_grad.astype(jnp.float32), axis=0)
    act_two_grad = jnp.dot(hidden_grad, full_up.T, preferred_element_type=jnp.float32)
    gain_two_grad = jnp.sum(act_two_grad * normal_two, axis=0)
    shift_two_grad = jnp.sum(act_two_grad, axis=0)
    mid_grad = grad_flat + norm_back(act_two_grad, normal_two, inverse_two, gain_two)
    mid_low = mid_grad.astype(jnp.bfloat16)
    proj_grad = jnp.dot(attn_own.T, mid_low, preferred_element_type=jnp.float32)
    proj_bias_grad = jnp.sum(mid_low.astype(jnp.float32), axis=0)
    attn_grad = jnp.dot(mid_low, full_proj.T, preferred_element_type=jnp.float32).astype(
        jnp.bfloat16
    )
    below_grad = passed_along(attn_grad[:sent], "seq", -1)
    grad_ext = jnp.concatenate([attn_grad[sent:], below_grad], axis=0)
    qkv_grad_ext, score_total = attend_back(qkv_ext, grad_ext, take, give, probs_low)
    table_grad = jnp.dot(
        score_total.reshape(head_count, SPAN * SPAN), one_hot, precision=lax.Precision.HIGHEST
    )
    above_grad = passed_along(qkv_grad_ext[kept:], "seq", 1)
    qkv_grad = jnp.concatenate([above_grad, qkv_grad_ext[:kept]], axis=0)
    qkv_weight_grad = jnp.dot(act_one.T, qkv_grad, preferred_element_type=jnp.float32)
    bias_sums = jnp.sum(qkv_grad.astype(jnp.float32), axis=0)
    act_one_grad = jnp.dot(qkv_grad, full_qkv.T, preferred_element_type=jnp.float32)
    gain_one_grad = jnp.sum(act_one_grad * normal_one, axis=0)
    shift_one_grad = jnp.sum(act_one_grad, axis=0)
    input_grad = mid_grad + norm_back(act_one_grad, normal_one, inverse_one, gain_one)
    vector_grad = jnp.concatenate(
        [
            gain_one_grad,
            shift_one_grad,
            bias_sums[0:model_width],
            bias_sums[2 * model_width : 3 * model_width],
            proj_bias_grad,
            gain_two_grad,
            shift_two_grad,
            down_bias_grad,
            up_bias_grad,
        ]
    )
    reduced, vector_sum, table_sum = summed(
        qkv_weight_grad, proj_grad, up_grad, down_grad, vector_grad, table_grad
    )
    qkv_new = adam_step(qkv_weight, qkv_first, qkv_second, reduced[0], matrix_rate, matrix_decay)
    proj_new = adam_step(
        proj_weight, proj_first, proj_second, reduced[1], matrix_rate, matrix_decay
    )
    up_new = adam_step(up_weight, up_first, up_second, reduced[2], matrix_rate, matrix_decay)
    down_new = adam_step(
        down_weight, down_first, down_second, reduced[3], matrix_rate, matrix_decay
    )
    vector_new = adam_step(vectors, vectors_first, vectors_second, vector_sum, vector_rate, 0.0)
    table_new = adam_step(bias_table, table_first, table_second, table_sum, vector_rate, 0.0)
    return (
        block_out.reshape(band_rows, band_cols, image_count, model_width).transpose(2, 0, 1, 3),
        input_grad.reshape(band_rows, band_cols, image_count, model_width).transpose(2, 0, 1, 3),
        qkv_new[0],
        qkv_new[1],
        qkv_new[2],
        proj_new[0],
        proj_new[1],
        proj_new[2],
        up_new[0],
        up_new[1],
        up_new[2],
        down_new[0],
        down_new[1],
        down_new[2],
        vector_new[0],
        vector_new[1],
        vector_new[2],
        table_new[0],
        table_new[1],
        table_new[2],
    )


def solution(mesh):
    placed = (
        P("fsdp", "seq", None, None),
        P("fsdp", "seq", None, None),
        P("seq", None),
        P(),
        P("fsdp", None),
        P("fsdp", None),
        P("fsdp", None),
        P("fsdp", None),
        P("fsdp", None),
        P("fsdp", None),
        P("fsdp", None),
        P("fsdp", None),
        P("fsdp", None),
        P("fsdp", None),
        P("fsdp", None),
        P("fsdp", None),
        P(),
        P(),
        P(),
        P(),
        P(),
        P(),
    )
    return jax.shard_map(
        local,
        mesh=mesh,
        in_specs=placed,
        out_specs=(
            P("fsdp", "seq", None, None),
            P("fsdp", "seq", None, None),
            P("fsdp", None),
            P("fsdp", None),
            P("fsdp", None),
            P("fsdp", None),
            P("fsdp", None),
            P("fsdp", None),
            P("fsdp", None),
            P("fsdp", None),
            P("fsdp", None),
            P("fsdp", None),
            P("fsdp", None),
            P("fsdp", None),
            P(),
            P(),
            P(),
            P(),
            P(),
            P(),
        ),
        check_vma=False,
    )
```

```python
import jax
import jax.numpy as jnp
import numpy as np
from jax import lax
from jax.experimental import pallas as pl
from jax.experimental.pallas import tpu as pltpu
from jax.sharding import PartitionSpec as P

HEAD_DIM = 32
WIN = 7
SHIFT = 3
STEP = 10


norm_eps = 1e-05
mask_fill = -100.0
beta_first = 0.9
beta_second = 0.999
adam_eps = 1e-08
matrix_rate = 0.05
vector_rate = 0.3
matrix_decay = 0.05
root_half = 0.7071067811865476
root_two_pi = 0.3989422804014327


def passed_along(block, axis, distance):
    devices = range(lax.axis_size(axis))
    route = [((i - distance) % len(devices), i) for i in devices]
    return lax.ppermute(block, axis, route)


def layer_norm(values, gain, offset):
    centred = values - jnp.mean(values, axis=-1, keepdims=True)
    inverse = lax.rsqrt(jnp.mean(centred * centred, axis=-1, keepdims=True) + norm_eps)
    normal = centred * inverse
    return (normal * gain + offset, normal, inverse)


def norm_back(grad_in, normal, inverse, gain):
    scaled = grad_in * gain
    centre = jnp.mean(scaled, axis=-1, keepdims=True)
    along = jnp.mean(scaled * normal, axis=-1, keepdims=True)
    return inverse * (scaled - centre - normal * along)


def adam_step(param, first, second, grad, rate, decay):
    new_first = beta_first * first + (1.0 - beta_first) * grad
    new_second = beta_second * second + (1.0 - beta_second) * grad * grad
    first_hat = new_first / (1.0 - beta_first**STEP)
    second_hat = new_second / (1.0 - beta_second**STEP)
    new_param = param - rate * (first_hat / (jnp.sqrt(second_hat) + adam_eps) + decay * param)
    return (new_param, new_first, new_second)


def chunk_list(qkv, proj, up, down, width):
    chunks = []
    for k in range(down.shape[0] // proj.shape[0]):
        chunks.append((down, None, k))
    for k in range(up.shape[1] // width):
        chunks.append((up, k * width, 0))
    chunks.append((proj, 0, 0))
    for k in range(qkv.shape[1] // width):
        chunks.append((qkv, k * width, 0))
    return chunks


def tail_kernel(
    proj, up, down, act, qkv_in, grad, take_ext, take_own, take_halo, give_own, give_halo, probs,
    o_qkv, o_proj, o_up, o_down, o_grad, o_table,
    qkv, halo_in, halo_out, halo_back, q_w, k_w, v_w, d_w, gq_w, gk_w, gv_w,
    from_core, to_x, from_x, to_y, from_y, mine, to_z, from_z,
    core_send, core_recv, x_send, x_recv, y_send, y_recv, z_send, z_recv,
    zg_send, zg_recv, yg_send, yg_recv, h_send, h_recv,
):
    f32, bf16 = jnp.float32, jnp.bfloat16
    seq, fsdp = lax.axis_index("seq"), lax.axis_index("fsdp")
    z, y = seq // 2, seq % 2
    x, core = fsdp // 2, fsdp % 2
    sib = {"seq": seq, "fsdp": x * 2 + (1 - core)}
    across = {"seq": seq, "fsdp": (1 - x) * 2 + core}
    beside = {"seq": z * 2 + (1 - y), "fsdp": fsdp}
    others = [(z + d) % 4 for d in (1, 2, 3)]
    along = [{"seq": o * 2 + y, "fsdp": fsdp} for o in others]
    bands = lax.axis_size("seq")
    above = {"seq": (seq + bands - 1) % bands, "fsdp": fsdp}
    below = {"seq": (seq + 1) % bands, "fsdp": fsdp}
    barrier = pltpu.get_barrier_semaphore()
    for dev in [sib, across, beside, above, below] + along:
        pl.semaphore_signal(barrier, inc=1, device_id=dev, device_id_type=pl.DeviceIdType.MESH)
    pl.semaphore_wait(barrier, 8)

    rows, width = o_proj.shape
    half, quarter = rows // 2, rows // 8
    ins = chunk_list(qkv, proj, up, down, width)
    outs = chunk_list(o_qkv, o_proj, o_up, o_down, width)
    count = len(ins)
    sends = []

    def send(src, dst, s_sem, r_sem, dev):
        copy = pltpu.make_async_remote_copy(
            src_ref=src, dst_ref=dst, send_sem=s_sem, recv_sem=r_sem,
            device_id=dev, device_id_type=pl.DeviceIdType.MESH,
        )
        copy.start()
        sends.append(copy)
        return copy

    def part(c, shard, off, n):
        ref, col, block = ins[c]
        if col is None:
            per = ref.shape[0] // 4
            return ref.at[pl.ds(pl.multiple_of(shard * per + block * rows + off, 16), n), :]
        return ref.at[pl.ds(pl.multiple_of(shard * rows + off, 16), n), col : col + width]

    def result(c, off, n):
        ref, col, block = outs[c]
        if col is None:
            return ref.at[pl.ds(pl.multiple_of(block * rows + off, 16), n), :]
        return ref.at[pl.ds(pl.multiple_of(off, 16), n), col : col + width]

    c_core, c_x, c_y, c_z, c_zg, c_yg = {}, {}, {}, {}, {}, {}
    early = count - qkv.shape[1] // width
    padded = halo_in.shape[0]
    halo = send(grad.at[0:padded], halo_in, h_send.at[0], h_recv.at[0], above)

    def stage_core(c):
        c_core[c] = [
            send(part(c, xx * 2 + (1 - core), 0, rows), from_core.at[c, xx],
                 core_send.at[c, xx], core_recv.at[c, xx], sib)
            for xx in (0, 1)
        ]

    def stage_x(c):
        for copy in c_core[c]:
            copy.wait_recv()
        total = part(c, (1 - x) * 2 + core, 0, rows)[...].astype(f32) + from_core[c, 1 - x].astype(f32)
        to_x[c] = total.astype(bf16)
        c_x[c] = send(to_x.at[c], from_x.at[c], x_send.at[c], x_recv.at[c], across)

    def three(c, off):
        here = pl.ds(pl.multiple_of(off, 16), half)
        return (
            part(c, x * 2 + core, off, half)[...].astype(f32)
            + from_core[c, x, here].astype(f32)
            + from_x[c, here].astype(f32)
        )

    def stage_y(c):
        c_x[c].wait_recv()
        to_y[c] = three(c, (1 - y) * half).astype(bf16)
        c_y[c] = send(to_y.at[c], from_y.at[c], y_send.at[c], y_recv.at[c], beside)

    def stage_z(c):
        c_y[c].wait_recv()
        total = three(c, y * half) + from_y[c].astype(f32)
        mine[c] = total
        to_z[c] = total.astype(bf16)
        c_z[c] = [
            send(to_z.at[c, pl.ds(pl.multiple_of(others[d] * quarter, 16), quarter)], from_z.at[c, d],
                 z_send.at[c, d], z_recv.at[c, d], along[d])
            for d in range(3)
        ]

    def stage_sum(c):
        for copy in c_z[c]:
            copy.wait_recv()
        total = mine[c, pl.ds(pl.multiple_of(z * quarter, 16), quarter)]
        for d in range(3):
            total = total + from_z[c, d].astype(f32)
        place = result(c, y * half + z * quarter, quarter)
        place[...] = total.astype(bf16)
        c_zg[c] = [
            send(place, place, zg_send.at[c, d], zg_recv.at[c, d], along[d]) for d in range(3)
        ]

    def stage_back(c):
        for copy in c_zg[c]:
            copy.wait_recv()
        place = result(c, y * half, half)
        c_yg[c] = send(place, place, yg_send.at[c], yg_recv.at[c], beside)

    def stage_end(c):
        c_yg[c].wait_recv()

    def attend_back_group(g):
        windows = take_own.shape[0] // SPAN
        heads = GROUP // HEAD_DIM
        tall = heads * SPAN
        scale = HEAD_DIM ** (-0.5)
        masks = head_masks()
        for i, ref in enumerate((q_w, k_w, v_w)):
            start = i * grad.shape[1] + g * GROUP
            ref[...] = dot_f32(take_ext[...], qkv_in[:, start : start + GROUP]).astype(bf16)
        lanes = slice(g * GROUP, (g + 1) * GROUP)
        d_w[...] = (
            dot_f32(take_own[...], grad[:, lanes]) + dot_f32(take_halo[...], halo_in[:, lanes])
        ).astype(bf16)

        def window(n, total):
            here = pl.ds(pl.multiple_of(n * SPAN, SPAN), SPAN)
            tall_q = spread(q_w[here, :], masks)
            tall_d = spread(d_w[here, :], masks)
            low = probs[g * windows + n]
            prob = low.astype(f32)
            gv_w[here, :] = dot_f32(low, tall_d, ((0,), (0,))).astype(bf16)
            prob_grad = dot_f32(tall_d, v_w[here, :], ((1,), (1,)))
            along_row = jnp.sum(prob * prob_grad, axis=-1, keepdims=True)
            score_low = (prob * (prob_grad - along_row)).astype(bf16)
            gq_w[here, :] = (merged(dot_f32(score_low, k_w[here, :]), masks) * scale).astype(bf16)
            gk_w[here, :] = (dot_f32(score_low, tall_q, ((0,), (0,))) * scale).astype(bf16)
            return total + score_low.astype(f32)

        o_table[g * tall : (g + 1) * tall, :] = lax.fori_loop(
            0, windows, window, jnp.zeros((tall, SPAN), f32), unroll=2
        )
        for i, ref in enumerate((gq_w, gk_w, gv_w)):
            start = i * grad.shape[1] + g * GROUP
            o_grad[:, start : start + GROUP] = dot_f32(give_own[...], ref[...]).astype(bf16)
            halo_out[:, start : start + GROUP] = dot_f32(give_halo[...], ref[...]).astype(bf16)

    stages = [stage_y, stage_z, stage_sum, stage_back, stage_end]

    def step(t):
        for s, stage in enumerate(stages):
            if 0 <= t - s < count:
                stage(t - s)

    for c in range(early):
        stage_core(c)
    for c in range(early):
        stage_x(c)
    halo.wait_recv()
    groups = grad.shape[1] // GROUP
    for g in range(groups):
        attend_back_group(g)
        if g == 0:
            step(0)
            step(1)
    back = send(halo_out, halo_back, h_send.at[1], h_recv.at[1], below)
    step(2)
    step(3)
    back.wait_recv()
    o_grad[0:padded, :] = (o_grad[0:padded, :].astype(f32) + halo_back[...].astype(f32)).astype(bf16)
    for c in range(early, count):
        col = (c - early) * width
        qkv[:, col : col + width] = dot_f32(
            act[...], o_grad[:, col : col + width], ((0,), (0,))
        ).astype(bf16)
        stage_core(c)
    step(4)
    for c in range(early, count):
        stage_x(c)
    for t in range(5, count + len(stages) - 1):
        step(t)
    for copy in sends:
        copy.wait_send()


def vec_kernel(vec, o_vec, v_keep, v_core, v_x, v_y, v_z, v_send, v_recv):
    seq, fsdp = lax.axis_index("seq"), lax.axis_index("fsdp")
    z, y = seq // 2, seq % 2
    x, core = fsdp // 2, fsdp % 2
    sib = {"seq": seq, "fsdp": x * 2 + (1 - core)}
    across = {"seq": seq, "fsdp": (1 - x) * 2 + core}
    beside = {"seq": z * 2 + (1 - y), "fsdp": fsdp}
    along = [{"seq": ((z + d) % 4) * 2 + y, "fsdp": fsdp} for d in (1, 2, 3)]
    barrier = pltpu.get_barrier_semaphore()
    for dev in [sib, across, beside] + along:
        pl.semaphore_signal(barrier, inc=1, device_id=dev, device_id_type=pl.DeviceIdType.MESH)
    pl.semaphore_wait(barrier, 6)
    sends = []

    def send(src, dst, i, dev):
        copy = pltpu.make_async_remote_copy(
            src_ref=src, dst_ref=dst, send_sem=v_send.at[i], recv_sem=v_recv.at[i],
            device_id=dev, device_id_type=pl.DeviceIdType.MESH,
        )
        copy.start()
        sends.append(copy)
        return copy

    send(vec, v_core, 0, sib).wait_recv()
    v_keep[0] = vec[...] + v_core[...]
    send(v_keep.at[0], v_x, 1, across).wait_recv()
    v_keep[1] = v_keep[0] + v_x[...]
    send(v_keep.at[1], v_y, 2, beside).wait_recv()
    v_z[z] = v_keep[1] + v_y[...]
    for copy in [send(v_z.at[z], v_z.at[z], 3 + d, along[d]) for d in range(3)]:
        copy.wait_recv()
    o_vec[...] = v_z[0] + v_z[1] + v_z[2] + v_z[3]
    for copy in sends:
        copy.wait_send()


def reduce_vec(vec):
    vmem = pl.BlockSpec(memory_space=pltpu.VMEM)
    dma = pltpu.SemaphoreType.DMA
    one = pltpu.VMEM(vec.shape, jnp.float32)
    return pl.pallas_call(
        vec_kernel,
        out_shape=jax.ShapeDtypeStruct(vec.shape, jnp.float32),
        in_specs=[vmem],
        out_specs=vmem,
        scratch_shapes=[
            pltpu.VMEM((2,) + vec.shape, jnp.float32), one, one, one,
            pltpu.VMEM((4,) + vec.shape, jnp.float32), dma((6,)), dma((6,)),
        ],
        compiler_params=pltpu.CompilerParams(
            collective_id=2, has_side_effects=True, vmem_limit_bytes=16 * 1024 * 1024
        ),
        name="reduce_vec",
    )(vec)


def tail(proj, up, down, act, qkv_ext, grad, take, sent, probs):
    bf16 = jnp.bfloat16
    rows, width = proj.shape[0] // 4, proj.shape[1]
    model = grad.shape[1]
    n = (qkv_ext.shape[1] * model + proj.size + up.size + down.size) // (4 * rows * width)
    tokens, positions = take.shape[1], take.shape[0]
    padded = -(-sent // 16) * 16
    take_own = jnp.pad(take[:, : tokens - sent], ((0, 0), (sent, 0)))
    take_halo = jnp.pad(take[:, tokens - sent :], ((0, 0), (0, padded - sent)))
    tall = GROUP // HEAD_DIM * SPAN
    dma = pltpu.SemaphoreType.DMA
    vmem = pl.BlockSpec(memory_space=pltpu.VMEM)
    owned = [(model // 4, qkv_ext.shape[1])] + [(a.shape[0] // 4, a.shape[1]) for a in (proj, up, down)]
    return pl.pallas_call(
        tail_kernel,
        out_shape=[jax.ShapeDtypeStruct(shape, bf16) for shape in owned]
        + [
            jax.ShapeDtypeStruct(qkv_ext.shape, bf16),
            jax.ShapeDtypeStruct((model // GROUP * tall, SPAN), jnp.float32),
        ],
        in_specs=[vmem] * 12,
        out_specs=[vmem] * 6,
        scratch_shapes=[
            pltpu.VMEM((model, qkv_ext.shape[1]), bf16),
            pltpu.VMEM((padded, model), bf16),
            pltpu.VMEM((padded, qkv_ext.shape[1]), bf16),
            pltpu.VMEM((padded, qkv_ext.shape[1]), bf16),
        ]
        + [pltpu.VMEM((positions, GROUP), bf16)] * 7
        + [
            pltpu.VMEM((n, 2, rows, width), bf16),
            pltpu.VMEM((n, rows, width), bf16),
            pltpu.VMEM((n, rows, width), bf16),
            pltpu.VMEM((n, rows // 2, width), bf16),
            pltpu.VMEM((n, rows // 2, width), bf16),
            pltpu.VMEM((n, rows // 2, width), jnp.float32),
            pltpu.VMEM((n, rows // 2, width), bf16),
            pltpu.VMEM((n, 3, rows // 8, width), bf16),
            dma((n, 2)), dma((n, 2)), dma((n,)), dma((n,)), dma((n,)), dma((n,)),
            dma((n, 3)), dma((n, 3)), dma((n, 3)), dma((n, 3)), dma((n,)), dma((n,)),
            dma((2,)), dma((2,)),
        ],
        compiler_params=pltpu.CompilerParams(
            collective_id=0, has_side_effects=True, vmem_limit_bytes=48 * 1024 * 1024
        ),
        name="tail",
    )(proj, up, down, act, qkv_ext, grad, take, take_own, take_halo, take_own.T, take_halo.T, probs)


def summed_vectors(vector_grad, table_grad):
    size = vector_grad.size + table_grad.size
    padded = -(-size // 1024) * 1024
    flat = jnp.concatenate(
        [vector_grad, table_grad.reshape(-1), jnp.zeros((padded - size,), jnp.float32)]
    ).reshape(padded // 128, 128)
    total = reduce_vec(flat).reshape(-1)
    return total[: vector_grad.size], total[vector_grad.size : size].reshape(table_grad.shape)


SPAN = 64
GROUP = 256


def gather_kernel(qkv, proj, o_qkv, o_proj, sib_send, sib_recv, x_send, x_recv, on_send, on_recv):
    seq, fsdp = lax.axis_index("seq"), lax.axis_index("fsdp")
    x, core = fsdp // 2, fsdp % 2
    sib = {"seq": seq, "fsdp": x * 2 + (1 - core)}
    away = (1 - x) * 2 + core
    across = {"seq": seq, "fsdp": away}
    barrier = pltpu.get_barrier_semaphore()
    for dev in (sib, across):
        pl.semaphore_signal(barrier, inc=1, device_id=dev, device_id_type=pl.DeviceIdType.MESH)
    rows, width = proj.shape
    places = [(o_qkv, k * width) for k in range(qkv.shape[1] // width)] + [(o_proj, 0)]
    own = pl.ds(pl.multiple_of(fsdp * rows, 16), rows)
    o_qkv[own, :] = qkv[...].astype(jnp.bfloat16)
    o_proj[own, :] = proj[...].astype(jnp.bfloat16)
    pl.semaphore_wait(barrier, 2)
    sends = []

    def send(i, shard, s_sem, r_sem, dev):
        ref, col = places[i]
        place = ref.at[pl.ds(pl.multiple_of(shard * rows, 16), rows), col : col + width]
        copy = pltpu.make_async_remote_copy(
            src_ref=place, dst_ref=place, send_sem=s_sem.at[i], recv_sem=r_sem.at[i],
            device_id=dev, device_id_type=pl.DeviceIdType.MESH,
        )
        copy.start()
        sends.append(copy)
        return copy

    count = len(places)
    first = [send(i, fsdp, x_send, x_recv, across) for i in range(count)]
    near = [send(i, fsdp, sib_send, sib_recv, sib) for i in range(count)]
    far = []
    for i in range(count):
        first[i].wait_recv()
        far.append(send(i, away, on_send, on_recv, sib))
    for copy in near + far:
        copy.wait_recv()
    for copy in sends:
        copy.wait_send()


def gather_first(qkv, proj):
    count = qkv.shape[1] // proj.shape[1] + 1
    vmem = pl.BlockSpec(memory_space=pltpu.VMEM)
    dma = pltpu.SemaphoreType.DMA
    return pl.pallas_call(
        gather_kernel,
        out_shape=[jax.ShapeDtypeStruct((4 * a.shape[0], a.shape[1]), jnp.bfloat16) for a in (qkv, proj)],
        in_specs=[vmem] * 2,
        out_specs=[vmem] * 2,
        scratch_shapes=[dma((count,))] * 6,
        compiler_params=pltpu.CompilerParams(
            collective_id=1, has_side_effects=True, vmem_limit_bytes=16 * 1024 * 1024
        ),
        name="gather_first",
    )(qkv, proj)


def head_masks():
    lane = lax.broadcasted_iota(jnp.int32, (SPAN, GROUP), 1) // HEAD_DIM
    return [lane == h for h in range(GROUP // HEAD_DIM)]


def spread(block, masks):
    return jnp.concatenate([jnp.where(m, block, jnp.zeros_like(block)) for m in masks], axis=0)


def merged(tall, masks):
    total = jnp.zeros((SPAN, GROUP), jnp.float32)
    for h, m in enumerate(masks):
        total = total + jnp.where(m, tall[h * SPAN : (h + 1) * SPAN], 0.0)
    return total


def dot_f32(a, b, dims=((1,), (0,))):
    return lax.dot_general(a, b, (dims, ((), ())), preferred_element_type=jnp.float32)


def attend_kernel(qkv, take, give, bias, mask, out, probs, q_w, k_w, v_w, o_w):
    bf16 = jnp.bfloat16
    width = out.shape[1]
    cols = mask.shape[0]
    windows = take.shape[0] // SPAN
    heads = GROUP // HEAD_DIM
    tall = heads * SPAN
    pad_key = lax.broadcasted_iota(jnp.int32, (1, SPAN), 1) >= WIN * WIN
    masks = head_masks()
    for g in range(width // GROUP):
        for i, ref in enumerate((q_w, k_w, v_w)):
            start = i * width + g * GROUP
            ref[...] = dot_f32(take[...], qkv[:, start : start + GROUP]).astype(bf16)
        shift = jnp.where(pad_key, -1e30, bias[g * tall : (g + 1) * tall, :])

        for n in range(windows):
            here = pl.ds(n * SPAN, SPAN)
            tall_q = spread(q_w[here, :], masks)
            scores = dot_f32(tall_q, k_w[here, :], ((1,), (1,))) * HEAD_DIM ** (-0.5) + shift
            scores = (scores.reshape(heads, SPAN, SPAN) + mask[n % cols][None]).reshape(tall, SPAN)
            grown = jnp.exp(scores - jnp.max(scores, axis=-1, keepdims=True))
            low = (grown / jnp.sum(grown, axis=-1, keepdims=True)).astype(bf16)
            probs[g * windows + n] = low
            o_w[here, :] = merged(dot_f32(low, v_w[here, :]), masks).astype(bf16)
        out[:, g * GROUP : (g + 1) * GROUP] = dot_f32(give[...], o_w[...]).astype(bf16)


def attend_back_kernel(qkv, grad, take, give, probs, out, table, q_w, k_w, v_w, d_w, gq_w, gk_w, gv_w):
    bf16 = jnp.bfloat16
    width = grad.shape[1]
    windows = take.shape[0] // SPAN
    heads = GROUP // HEAD_DIM
    tall = heads * SPAN
    scale = HEAD_DIM ** (-0.5)
    masks = head_masks()
    for g in range(width // GROUP):
        for i, ref in enumerate((q_w, k_w, v_w)):
            start = i * width + g * GROUP
            ref[...] = dot_f32(take[...], qkv[:, start : start + GROUP]).astype(bf16)
        d_w[...] = dot_f32(take[...], grad[:, g * GROUP : (g + 1) * GROUP]).astype(bf16)
        total = jnp.zeros((tall, SPAN), jnp.float32)
        for n in range(windows):
            here = pl.ds(n * SPAN, SPAN)
            tall_q = spread(q_w[here, :], masks)
            tall_d = spread(d_w[here, :], masks)
            low = probs[g * windows + n]
            prob = low.astype(jnp.float32)
            gv_w[here, :] = dot_f32(low, tall_d, ((0,), (0,))).astype(bf16)
            prob_grad = dot_f32(tall_d, v_w[here, :], ((1,), (1,)))
            along = jnp.sum(prob * prob_grad, axis=-1, keepdims=True)
            score_low = (prob * (prob_grad - along)).astype(bf16)
            total = total + score_low.astype(jnp.float32)
            gq_w[here, :] = (merged(dot_f32(score_low, k_w[here, :]), masks) * scale).astype(bf16)
            gk_w[here, :] = (dot_f32(score_low, tall_q, ((0,), (0,))) * scale).astype(bf16)
        table[g * tall : (g + 1) * tall, :] = total
        for i, ref in enumerate((gq_w, gk_w, gv_w)):
            start = i * width + g * GROUP
            out[:, start : start + GROUP] = dot_f32(give[...], ref[...]).astype(bf16)


def window_places(rows, cols, images):
    place = np.zeros((images * (cols // WIN) * SPAN, rows * cols * images), np.float32)
    for image in range(images):
        for w in range(cols // WIN):
            for r in range(rows):
                for c in range(WIN):
                    token = (r * cols + (w * WIN + c + SHIFT) % cols) * images + image
                    place[(image * (cols // WIN) + w) * SPAN + r * WIN + c, token] = 1.0
    return jnp.asarray(place, jnp.bfloat16)


def attend(qkv, take, give, bias, mask):
    tokens, width = qkv.shape[0], qkv.shape[1] // 3
    groups, windows = width // GROUP, take.shape[0] // SPAN
    tall = GROUP // HEAD_DIM * SPAN
    vmem = pl.BlockSpec(memory_space=pltpu.VMEM)
    return pl.pallas_call(
        attend_kernel,
        out_shape=[
            jax.ShapeDtypeStruct((tokens, width), jnp.bfloat16),
            jax.ShapeDtypeStruct((groups * windows, tall, SPAN), jnp.bfloat16),
        ],
        in_specs=[vmem] * 5,
        out_specs=[vmem] * 2,
        scratch_shapes=[pltpu.VMEM((take.shape[0], GROUP), jnp.bfloat16)] * 4,
        compiler_params=pltpu.CompilerParams(vmem_limit_bytes=32 * 1024 * 1024),
        name="attend",
    )(qkv, take, give, bias, mask)


def attend_back(qkv, grad, take, give, probs):
    tall = GROUP // HEAD_DIM * SPAN
    vmem = pl.BlockSpec(memory_space=pltpu.VMEM)
    return pl.pallas_call(
        attend_back_kernel,
        out_shape=[
            jax.ShapeDtypeStruct(qkv.shape, jnp.bfloat16),
            jax.ShapeDtypeStruct((grad.shape[1] // GROUP * tall, SPAN), jnp.float32),
        ],
        in_specs=[vmem] * 5,
        out_specs=[vmem] * 2,
        scratch_shapes=[pltpu.VMEM((take.shape[0], GROUP), jnp.bfloat16)] * 7,
        compiler_params=pltpu.CompilerParams(vmem_limit_bytes=32 * 1024 * 1024),
        name="attend_back",
    )(qkv, grad, take, give, probs)


def local(
    inputs,
    out_grad,
    regions,
    rel_index,
    qkv_weight,
    qkv_first,
    qkv_second,
    proj_weight,
    proj_first,
    proj_second,
    up_weight,
    up_first,
    up_second,
    down_weight,
    down_first,
    down_second,
    vectors,
    vectors_first,
    vectors_second,
    bias_table,
    table_first,
    table_second,
):
    image_count, band_rows, band_cols, model_width = inputs.shape
    hidden_width = up_weight.shape[1]
    head_count = model_width // HEAD_DIM
    window_cols = band_cols // WIN
    token_count = image_count * band_rows * band_cols
    gain_one = vectors[0:model_width]
    shift_one = vectors[model_width : 2 * model_width]
    query_bias = vectors[2 * model_width : 3 * model_width]
    value_bias = vectors[3 * model_width : 4 * model_width]
    proj_bias = vectors[4 * model_width : 5 * model_width]
    gain_two = vectors[5 * model_width : 6 * model_width]
    shift_two = vectors[6 * model_width : 7 * model_width]
    down_bias = vectors[7 * model_width : 8 * model_width]
    up_bias = vectors[8 * model_width : 8 * model_width + hidden_width]
    direct = lax.axis_size("seq") == 8 and lax.axis_size("fsdp") == 4
    up_next, down_next = up_weight, down_weight
    if direct:
        full_qkv, full_proj = gather_first(qkv_weight, proj_weight)
        full_qkv, full_proj, up_next, down_next = lax.optimization_barrier(
            (full_qkv, full_proj, up_weight, down_weight)
        )
    else:
        full_qkv = lax.all_gather(qkv_weight.astype(jnp.bfloat16), "fsdp", axis=0, tiled=True)
        full_proj = lax.all_gather(proj_weight.astype(jnp.bfloat16), "fsdp", axis=0, tiled=True)
    full_up = lax.all_gather(up_next.astype(jnp.bfloat16), "fsdp", axis=0, tiled=True)
    full_down = lax.all_gather(down_next.astype(jnp.bfloat16), "fsdp", axis=0, tiled=True)
    sent = SHIFT * band_cols * image_count
    kept = token_count - sent
    flat_in = inputs.transpose(1, 2, 0, 3).reshape(token_count, model_width)
    normed_one, normal_one, inverse_one = layer_norm(flat_in, gain_one, shift_one)
    act_one = normed_one.astype(jnp.bfloat16)
    qkv_bias = jnp.concatenate([query_bias, jnp.zeros_like(query_bias), value_bias])
    qkv_vals = (jnp.dot(act_one, full_qkv, preferred_element_type=jnp.float32) + qkv_bias).astype(
        jnp.bfloat16
    )
    below = passed_along(qkv_vals[:sent], "seq", -1)
    qkv_ext = jnp.concatenate([qkv_vals[sent:], below], axis=0)
    pairs = rel_index.shape[0]
    table_size = bias_table.shape[1]
    rel_padded = jnp.pad(rel_index, ((0, SPAN - pairs), (0, SPAN - pairs)), constant_values=-1)
    one_hot = (
        rel_padded.reshape(-1)[:, None] == jnp.arange(table_size, dtype=jnp.int32)[None, :]
    ).astype(jnp.float32)
    position_bias = jnp.dot(bias_table, one_hot.T, precision=lax.Precision.HIGHEST).reshape(
        head_count * SPAN, SPAN
    )
    labels = (
        regions.reshape(band_rows, window_cols, WIN).transpose(1, 0, 2).reshape(window_cols, pairs)
    )
    labels = jnp.pad(labels, ((0, 0), (0, SPAN - pairs)), constant_values=-1)
    mask_bias = jnp.where(labels[:, :, None] == labels[:, None, :], 0.0, mask_fill).astype(
        jnp.float32
    )
    take = window_places(band_rows, band_cols, image_count)
    give = take.T
    attended, probs_low = attend(qkv_ext, take, give, position_bias, mask_bias)
    above = passed_along(attended[kept:], "seq", 1)
    attn_own = jnp.concatenate([above, attended[:kept]], axis=0)
    mid = flat_in + (jnp.dot(attn_own, full_proj, preferred_element_type=jnp.float32) + proj_bias)
    normed_two, normal_two, inverse_two = layer_norm(mid, gain_two, shift_two)
    act_two = normed_two.astype(jnp.bfloat16)
    hidden = jnp.dot(act_two, full_up, preferred_element_type=jnp.float32) + up_bias
    gelu_low = jax.nn.gelu(hidden, approximate=False).astype(jnp.bfloat16)
    block_out = mid + (jnp.dot(gelu_low, full_down, preferred_element_type=jnp.float32) + down_bias)
    grad_flat = out_grad.transpose(1, 2, 0, 3).reshape(token_count, model_width)
    grad_low = grad_flat.astype(jnp.bfloat16)
    down_grad = jnp.dot(gelu_low.T, grad_low, preferred_element_type=jnp.float32)
    down_bias_grad = jnp.sum(grad_low.astype(jnp.float32), axis=0)
    slope = (
        0.5 * (1.0 + lax.erf(hidden * root_half))
        + hidden * jnp.exp(-0.5 * hidden * hidden) * root_two_pi
    )
    hidden_grad = (
        jnp.dot(grad_low, full_down.T, preferred_element_type=jnp.float32) * slope
    ).astype(jnp.bfloat16)
    up_grad = jnp.dot(act_two.T, hidden_grad, preferred_element_type=jnp.float32)
    up_bias_grad = jnp.sum(hidden_grad.astype(jnp.float32), axis=0)
    act_two_grad = jnp.dot(hidden_grad, full_up.T, preferred_element_type=jnp.float32)
    gain_two_grad = jnp.sum(act_two_grad * normal_two, axis=0)
    shift_two_grad = jnp.sum(act_two_grad, axis=0)
    mid_grad = grad_flat + norm_back(act_two_grad, normal_two, inverse_two, gain_two)
    mid_low = mid_grad.astype(jnp.bfloat16)
    proj_grad = jnp.dot(attn_own.T, mid_low, preferred_element_type=jnp.float32)
    proj_bias_grad = jnp.sum(mid_low.astype(jnp.float32), axis=0)
    attn_grad = jnp.dot(mid_low, full_proj.T, preferred_element_type=jnp.float32).astype(
        jnp.bfloat16
    )
    if direct:
        *owned, qkv_grad, score_total = tail(
            proj_grad.astype(jnp.bfloat16), up_grad.astype(jnp.bfloat16), down_grad.astype(jnp.bfloat16),
            act_one, qkv_ext, attn_grad, take, sent, probs_low,
        )
    else:
        below_grad = passed_along(attn_grad[:sent], "seq", -1)
        grad_ext = jnp.concatenate([attn_grad[sent:], below_grad], axis=0)
        qkv_grad_ext, score_total = attend_back(qkv_ext, grad_ext, take, give, probs_low)
        above_grad = passed_along(qkv_grad_ext[kept:], "seq", 1)
        qkv_grad = jnp.concatenate([above_grad, qkv_grad_ext[:kept]], axis=0)
        qkv_weight_grad = jnp.dot(act_one.T, qkv_grad, preferred_element_type=jnp.float32)
        owned = [
            lax.psum(
                lax.psum_scatter(g.astype(jnp.bfloat16), "fsdp", scatter_dimension=0, tiled=True), "seq"
            )
            for g in (qkv_weight_grad, proj_grad, up_grad, down_grad)
        ]
    reduced = [g.astype(jnp.float32) for g in owned]
    table_grad = jnp.dot(
        score_total.reshape(head_count, SPAN * SPAN), one_hot, precision=lax.Precision.HIGHEST
    )
    bias_sums = jnp.sum(qkv_grad.astype(jnp.float32), axis=0)
    act_one_grad = jnp.dot(qkv_grad, full_qkv.T, preferred_element_type=jnp.float32)
    gain_one_grad = jnp.sum(act_one_grad * normal_one, axis=0)
    shift_one_grad = jnp.sum(act_one_grad, axis=0)
    input_grad = mid_grad + norm_back(act_one_grad, normal_one, inverse_one, gain_one)
    vector_grad = jnp.concatenate(
        [
            gain_one_grad,
            shift_one_grad,
            bias_sums[0:model_width],
            bias_sums[2 * model_width : 3 * model_width],
            proj_bias_grad,
            gain_two_grad,
            shift_two_grad,
            down_bias_grad,
            up_bias_grad,
        ]
    )
    if direct:
        vector_sum, table_sum = summed_vectors(vector_grad, table_grad)
    else:
        vector_sum, table_sum = lax.psum((vector_grad, table_grad), ("seq", "fsdp"))
    qkv_new = adam_step(qkv_weight, qkv_first, qkv_second, reduced[0], matrix_rate, matrix_decay)
    proj_new = adam_step(
        proj_weight, proj_first, proj_second, reduced[1], matrix_rate, matrix_decay
    )
    up_new = adam_step(up_weight, up_first, up_second, reduced[2], matrix_rate, matrix_decay)
    down_new = adam_step(
        down_weight, down_first, down_second, reduced[3], matrix_rate, matrix_decay
    )
    vector_new = adam_step(vectors, vectors_first, vectors_second, vector_sum, vector_rate, 0.0)
    table_new = adam_step(bias_table, table_first, table_second, table_sum, vector_rate, 0.0)
    return (
        block_out.reshape(band_rows, band_cols, image_count, model_width).transpose(2, 0, 1, 3),
        input_grad.reshape(band_rows, band_cols, image_count, model_width).transpose(2, 0, 1, 3),
        qkv_new[0],
        qkv_new[1],
        qkv_new[2],
        proj_new[0],
        proj_new[1],
        proj_new[2],
        up_new[0],
        up_new[1],
        up_new[2],
        down_new[0],
        down_new[1],
        down_new[2],
        vector_new[0],
        vector_new[1],
        vector_new[2],
        table_new[0],
        table_new[1],
        table_new[2],
    )


def solution(mesh):
    placed = (
        P("fsdp", "seq", None, None),
        P("fsdp", "seq", None, None),
        P("seq", None),
        P(),
        P("fsdp", None),
        P("fsdp", None),
        P("fsdp", None),
        P("fsdp", None),
        P("fsdp", None),
        P("fsdp", None),
        P("fsdp", None),
        P("fsdp", None),
        P("fsdp", None),
        P("fsdp", None),
        P("fsdp", None),
        P("fsdp", None),
        P(),
        P(),
        P(),
        P(),
        P(),
        P(),
    )
    return jax.shard_map(
        local,
        mesh=mesh,
        in_specs=placed,
        out_specs=(
            P("fsdp", "seq", None, None),
            P("fsdp", "seq", None, None),
            P("fsdp", None),
            P("fsdp", None),
            P("fsdp", None),
            P("fsdp", None),
            P("fsdp", None),
            P("fsdp", None),
            P("fsdp", None),
            P("fsdp", None),
            P("fsdp", None),
            P("fsdp", None),
            P("fsdp", None),
            P("fsdp", None),
            P(),
            P(),
            P(),
            P(),
            P(),
            P(),
        ),
        check_vma=False,
    )
```
